512 devices in a mesh: tm: 64 (over x, z), mp: 8 (over y, core).
Axes of the slice: x: 4, y: 4, z: 16, core: 2. Of those that a mesh axis runs over, the one named last changes fastest.
Arguments:
- observations: bfloat16 [64, 4096, 256], P('tm', None, 'mp'), may hold values from -6 to 6
- contact: int32 [512, 8, 8], P('tm'), may hold values 0 or 1
- resets: int32 [8, 4096], P(None, 'tm'), may hold values 0 or 1
- q_weight: bfloat16 [2048, 1024], P(None, 'mp'), may hold values from -0.125 to 0.125
- k_weight: bfloat16 [2048, 1024], P(None, 'mp'), may hold values from -0.125 to 0.125
- v_weight: bfloat16 [2048, 1024], P(None, 'mp'), may hold values from -0.125 to 0.125
- decay_weight: bfloat16 [2048, 1024], P(None, 'mp'), may hold values from -0.125 to 0.125
- gate_weight: bfloat16 [2048, 1024], P(None, 'mp'), may hold values from -0.125 to 0.125
- decay_bias: float32 [8, 128], P('mp'), may hold values from 4 to 14
- norm_gain: float32 [8, 128], P('mp'), may hold values from 0.25 to 1.75
- out_weight: bfloat16 [1024, 2048], P(None, 'mp'), may hold values from -0.1875 to 0.1875
- out_cotangent: bfloat16 [8, 4096, 2048], P(None, 'tm', 'mp'), may hold values from -0.03125 to 0.03125
Outputs:
- following_frame: bfloat16 [8, 4096, 2048], P(None, 'tm', 'mp')
- out_weight_grad: float32 [1024, 2048], P('tm', 'mp')
The draws below stay inside these ranges and needn't reach their ends.
All inputs are finite; a program needn't handle non-finite values. No bound on the sum of `contact` or of `resets` on one device may be relied on, other than what follows from the above.
Results may differ from the reference program's by a relative error of at most 0.0049.
Values may be sent and summed in bfloat16 or wider, within the bound.
A program may use at most 128 MiB of HBM per device.

```python
import math
import jax
import jax.numpy as jnp
from jax import lax

D = 2048
HEADS = 8
HK = 128
HV = 128
CH = 8
CB = 8
FR_DEV = 64
FRAMES = 4096
SPLITS = 8


def draw_decay_bias(key, part):
    drawn = jnp.exp(jax.random.uniform(key, (HEADS, HK), jnp.float32, math.log(4.0), math.log(14.0)))
    return drawn


def plant(result, own_key, low, largest):
    shape = result.shape
    spot = [jax.random.randint(jax.random.fold_in(own_key, axis), (), 0, shape[axis]) for axis in range(len(shape))]
    result = result.at[tuple(spot)].set(low)
    longest = shape.index(max(shape))
    spot[longest] = (spot[longest] + 1) % shape[longest]
    return result.at[tuple(spot)].set(largest)


def level_of(rng, dims, split, smallest, top_value):
    def one(dim, shards_of):
        heights = jax.random.uniform(jax.random.fold_in(jax.random.fold_in(rng, 6), dim), (shards_of,), jnp.float32, smallest / len(split), top_value / len(split))
        return jnp.repeat(jnp.exp(heights), dims[dim] // shards_of).reshape((-1,) + (1,) * (len(dims) - dim - 1))

    factor_of = one(*split[0])
    for cut in split[1:]:
        factor_of = factor_of * one(*cut)
    return factor_of


def bell_draw(rng, dims, width, reach, cuts=(), dtype=jnp.bfloat16):
    loudness = level_of(rng, dims, cuts, -0.22, 0.18) if cuts else 1.0
    result = jax.random.normal(rng, dims, jnp.float32) * width * loudness
    return jnp.minimum(jnp.maximum(result, -reach), reach).astype(dtype)


def setup_inputs(seed: int = 0) -> dict:
    key_list = jax.random.split(jax.random.key(seed), 13)
    observations = bell_draw(key_list[0], (CH * SPLITS, FRAMES, D // SPLITS), 1.0, 6.0, ((0, 64), (2, 8)))
    contact = plant((jax.random.randint(key_list[1], (FRAMES // CB, CH, CH), 0, 4) < 1).astype(jnp.int32), jax.random.fold_in(key_list[1], 1), 0, 1)
    resets = plant((jax.random.randint(key_list[2], (CH, FRAMES), 0, FRAMES) < 1).astype(jnp.int32), jax.random.fold_in(key_list[2], 1), 0, 1)
    q_weight = bell_draw(key_list[3], (D, HEADS * HK), D ** -0.5, 0.125, ((1, 8),))
    k_weight = bell_draw(key_list[4], (D, HEADS * HK), D ** -0.5, 0.125, ((1, 8),))
    v_weight = bell_draw(key_list[5], (D, HEADS * HV), D ** -0.5, 0.125, ((1, 8),))
    decay_weight = bell_draw(key_list[6], (D, HEADS * HK), D ** -0.5, 0.125, ((1, 8),))
    gate_weight = bell_draw(key_list[7], (D, HEADS * HV), D ** -0.5, 0.125, ((1, 8),))
    decay_bias = draw_decay_bias(jax.random.fold_in(key_list[12], 71), 0)
    norm_gain = jnp.clip(1.0 + 0.15 * jax.random.normal(key_list[9], (HEADS, HV), jnp.float32), 0.25, 1.75)
    out_weight = bell_draw(key_list[10], (HEADS * HV, D), (HEADS * HV) ** -0.5, 0.1875, ((1, 8),))
    out_cotangent = bell_draw(key_list[11], (CH, FRAMES, D), ((CH * FRAMES) ** -0.5), 0.03125, ((1, 64), (2, 8)))
    return dict(observations=observations, contact=contact, resets=resets, q_weight=q_weight, k_weight=k_weight, v_weight=v_weight, decay_weight=decay_weight, gate_weight=gate_weight, decay_bias=decay_bias, norm_gain=norm_gain, out_weight=out_weight, out_cotangent=out_cotangent)


def intra_char(arrays):
    queries, key_rows, value_rows, log_total, resets_observed = arrays
    frames = queries.shape[0]
    row_index = lax.broadcasted_iota(jnp.int32, (frames, frames), 0)
    earlier = lax.broadcasted_iota(jnp.int32, (frames, frames), 1)
    causal = (row_index >= earlier) & (resets_observed[:, None] == resets_observed[None, :])
    gap_log = jnp.minimum(log_total[:, None] - log_total[None, :], 0.0)
    pair_decay = jnp.where(causal[:, :, None, None], jnp.exp(gap_log), 0.0)
    scores = jnp.einsum('thk,shk,tshk->tsh', queries, key_rows, pair_decay, precision=lax.Precision.HIGHEST)
    return jnp.einsum('tsh,shv->thv', scores, value_rows, precision=lax.Precision.HIGHEST)

def block_terms(queries, key_rows, value_rows, log_decay, reset_block):
    log_total = jnp.cumsum(log_decay, axis=1)
    resets_observed = jnp.cumsum(reset_block, axis=1)
    last_total = log_total[:, -1]
    last_seen = resets_observed[:, -1]
    untouched = (resets_observed == 0).astype(jnp.float32)
    survives = (resets_observed == last_seen[:, None]).astype(jnp.float32)
    block_decay = jnp.exp(last_total) * (last_seen == 0).astype(jnp.float32)[:, None, None]
    weights = jnp.exp(last_total[:, None] - log_total) * survives[:, :, None, None]
    block_state = jnp.einsum('cthk,cthv->chkv', key_rows * weights, value_rows, precision=lax.Precision.HIGHEST)
    carried_q = queries * jnp.exp(log_total) * untouched[:, :, None, None]
    inside = lax.map(intra_char, (queries, key_rows, value_rows, log_total, resets_observed))
    return (block_decay, block_state, carried_q, inside)

def finish(attended, gate_values, gain_head, links_block):
    characters, frames, head_count, value_width = attended.shape
    blocks = links_block.shape[0]
    mean_square = lax.optimization_barrier(jnp.mean(attended * attended, axis=-1, keepdims=True))
    normed = attended * lax.rsqrt(mean_square + 1e-06) * gain_head
    regrouped_rows = normed.reshape(characters, blocks, frames // blocks * head_count * value_width)
    contact_factor = links_block.astype(jnp.float32)
    total_rows = jnp.einsum('nmr,rnd->mnd', contact_factor, regrouped_rows, precision=lax.Precision.HIGHEST)
    partners = jnp.maximum(lax.optimization_barrier(jnp.sum(contact_factor, axis=-1)), 1.0)
    mixed_rows = regrouped_rows + total_rows / jnp.transpose(partners)[:, :, None]
    mixed_rows = mixed_rows.reshape(characters, frames, head_count * value_width)
    return (mixed_rows * jax.nn.silu(gate_values)).astype(jnp.bfloat16)

def reference(observations, contact, resets, q_weight, k_weight, v_weight, decay_weight, gate_weight, decay_bias, norm_gain, out_weight, out_cotangent):
    splits = observations.shape[0] // CH
    features = observations.reshape(CH, splits, FRAMES, D // splits).transpose(0, 2, 1, 3).reshape(CH, FRAMES, D)
    blocks = FRAMES // FR_DEV
    obs_blocks = features.reshape(CH, blocks, FR_DEV, D).transpose(1, 0, 2, 3)
    reset_blocks = resets.reshape(CH, blocks, FR_DEV).transpose(1, 0, 2)
    link_blocks = contact.reshape(blocks, FR_DEV // CB, CH, CH)

    def advance(carried, arrays):
        obs_block, reset_block, links_block = arrays
        row_block = obs_block.reshape(CH * FR_DEV, D)

        def project(matrix):
            return jnp.dot(row_block, matrix, preferred_element_type=jnp.float32).reshape(CH, FR_DEV, HEADS, -1)
        queries = project(q_weight) * HK ** (-0.5)
        key_rows = project(k_weight)
        value_rows = project(v_weight)
        log_decay = jax.nn.log_sigmoid(project(decay_weight) + decay_bias)
        gate_values = jnp.dot(row_block, gate_weight, preferred_element_type=jnp.float32).reshape(CH, FR_DEV, HEADS * HV)
        block_decay, block_state, carried_q, inside = block_terms(queries, key_rows, value_rows, log_decay, reset_block)
        attended = inside + jnp.einsum('cthk,chkv->cthv', carried_q, carried, precision=lax.Precision.HIGHEST)
        carried = block_decay[..., None] * carried + block_state
        return (carried, finish(attended, gate_values, norm_gain, links_block))
    initial = jnp.zeros((CH, HEADS, HK, HV), jnp.float32)
    _, gated = lax.scan(advance, initial, (obs_blocks, reset_blocks, link_blocks))
    gated_rows = gated.transpose(1, 0, 2, 3).reshape(CH * FRAMES, HEADS * HV)
    following_frame = jnp.dot(gated_rows, out_weight, preferred_element_type=jnp.float32).astype(jnp.bfloat16).reshape(CH, FRAMES, D)
    cotangent_rows = out_cotangent.reshape(CH * FRAMES, D)
    weight_grad = lax.dot_general(gated_rows, cotangent_rows, (((0,), (0,)), ((), ())), preferred_element_type=jnp.float32)
    return (following_frame, weight_grad)
```

```python
import jax
import jax.numpy as jnp
from jax import lax
from jax.experimental import pallas as pl
from jax.experimental.pallas import tpu as pltpu
from jax.sharding import PartitionSpec as P

MESH = pl.DeviceIdType.MESH
BF = jnp.bfloat16
F32 = jnp.float32

HK = 128
CH = 8
TM, MP = 64, 8
NX, NZ, NY = 4, 16, 4
FR = 64
ROWS = CH * FR
LEVELS = (32, 16, 8, 4, 2, 1)


def dot(a, b, dims=((1,), (0,))):
    return lax.dot_general(a, b, (dims, ((), ())), preferred_element_type=F32)


def split(a):
    high = a.astype(BF)
    return high, (a - high.astype(F32)).astype(BF)


def dot3(a, b, dims=((1,), (0,))):
    ah, al = split(a)
    bh, bl = split(b)
    da, db = dims[0][0], dims[1][0]
    return dot(jnp.concatenate([ah, al, ah], da), jnp.concatenate([bh, bh, bl], db), dims)


def iota(shape, dim):
    return lax.broadcasted_iota(jnp.int32, shape, dim)


def kernel(
    obs, contact, resets, wq, wk, wv, wd, wg, bias, gain, ow, cot,
    out, grad,
    obs_v, con_v, res_v, w_v, bias_v, gain_v, ow_v, cot_v,
    pack, rx, feat, proj, decay_log, rcol, rrow, masks, sel, mix, inv_partners,
    sbuf, dbuf, st_in, d_in, d_t, pre, s_in, attended, carried_q, silu,
    gat, oacc, gradf, gbuf, xr, zf, zbuf, zr, out_v, grad_v,
    in_sem, w_sem, out_sem, a_sem, f_send, f_recv, st_sem, dk_sem, p_sem, g_send, g_recv, x_sem, z_sem,
):
    T = lax.axis_index("tm")
    M = lax.axis_index("mp")
    x, z = T // NZ, lax.rem(T, NZ)
    y, core = M // 2, lax.rem(M, 2)
    right_y, left_y, opp_y = lax.rem(y + 1, NY), lax.rem(y + 3, NY), lax.rem(y + 2, NY)

    def load(src, dst, i):
        return pltpu.make_async_copy(src, dst, in_sem.at[i])

    loads = [
        load(obs, obs_v, 0), load(contact, con_v, 1), load(resets, res_v, 2), load(bias, bias_v, 3),
        load(gain, gain_v, 4), load(ow, ow_v, 5), load(cot, cot_v, 6),
    ]
    loads[0].start()

    barrier = pltpu.get_barrier_semaphore()

    @pl.loop(1, TM)
    def _(k):
        pl.semaphore_signal(barrier, inc=1, device_id=(lax.rem(T + k, TM), M), device_id_type=MESH)

    sib = 2 * y + 1 - core
    right, left, opp = 2 * right_y + core, 2 * left_y + core, 2 * opp_y + core
    for other in (sib, right, left):
        pl.semaphore_signal(barrier, inc=1, device_id=(T, other), device_id_type=MESH)

    for one in loads[1:]:
        one.start()

    @pl.loop(0, MP)
    def _(m):
        for j, w in enumerate((wq, wk, wv, wd, wg)):
            for fh in range(2):
                pltpu.make_async_copy(
                    w.at[:, m, fh], w_v.at[m, fh, :, :, pl.ds(j * 128, 128)], w_sem
                ).start()

    loads[0].wait()
    low = iota((16, 128), 1) < 64

    @pl.loop(0, TM // 2)
    def _(u):
        tile = obs_v[:, pl.ds(pl.multiple_of(u * 128, 128), 128)].astype(F32)
        a, b = tile[:16], tile[16:]
        pack[2 * u] = jnp.where(low, a, pltpu.roll(b, 64, 1)).astype(BF)
        pack[2 * u + 1] = jnp.where(low, pltpu.roll(a, 64, 1), b).astype(BF)

    pl.semaphore_wait(barrier, TM - 1 + 3)

    def piece(src, dst, sems, peer):
        return pltpu.make_async_remote_copy(
            src_ref=src, dst_ref=dst, send_sem=sems.at[0], recv_sem=sems.at[1],
            device_id=(peer, M), device_id_type=MESH,
        )

    def wait_bytes(ref, sem):
        pltpu.make_async_copy(ref, ref, sem).wait()

    @pl.loop(1, TM)
    def _(k):
        peer = lax.rem(T + k, TM)
        piece(pack.at[peer], rx.at[T], a_sem, peer).start()

    rx[T] = pack[T]

    for one in loads[1:]:
        one.wait()
    tri = (iota((FR, FR), 0) >= iota((FR, FR), 1)).astype(BF)
    res = res_v[...].astype(F32).astype(BF)
    seen_col = dot(tri, res, ((1,), (1,)))
    seen_row = dot(res, tri, ((1,), (1,)))
    for c in range(CH):
        rcol[c] = jnp.broadcast_to(seen_col[:, c : c + 1], (FR, 128))
        rrow[c] = seen_row[c : c + 1, :]
    t_id, s_id = iota((FR, FR), 0), iota((FR, FR), 1)
    for i, h in enumerate(LEVELS):
        masks[i] = ((t_id // (2 * h) == s_id // (2 * h)) & (t_id // h > s_id // h)).astype(F32)
        sel[i * FR : (i + 1) * FR] = (s_id == (t_id // (2 * h)) * (2 * h) + h - 1).astype(BF)
    masks[len(LEVELS)] = (t_id == s_id).astype(F32)

    row_q, col_q = iota((ROWS, FR), 0), iota((ROWS, FR), 1)
    pick = (((row_q % FR) // 8) * 8 + row_q // FR == col_q).astype(BF)
    con = con_v[...].astype(F32).astype(BF)
    taken = dot(pick, con).astype(BF)
    inv_partners[...] = 1.0 / jnp.maximum(dot(taken, jnp.ones((CH, 128), BF)), 1.0)
    spread = (iota((CH, ROWS), 1) // FR == iota((CH, ROWS), 0)).astype(BF)
    same = iota((ROWS, ROWS), 0) % FR == iota((ROWS, ROWS), 1) % FR
    mix[...] = jnp.where(same, dot(taken, spread), 0.0).astype(BF)

    wait_bytes(rx.at[pl.ds(0, TM - 1)], a_sem.at[1])
    for c in range(CH):
        turned = rx[c * 8 : (c + 1) * 8].reshape(128, 128).T
        feat[M, c * FR : (c + 1) * FR, 0:128] = turned[:FR]
        feat[M, c * FR : (c + 1) * FR, 128:256] = turned[FR:]

    def gather(buf, send, recv, use):
        half = ROWS // 2

        def part(slot, h, i, to):
            ref = buf.at[slot, pl.ds(h * half, half)]
            return pltpu.make_async_remote_copy(
                src_ref=ref, dst_ref=ref, send_sem=send.at[i], recv_sem=recv.at[i],
                device_id=(T, to), device_id_type=MESH,
            )

        sent = []

        def go(*args):
            one = part(*args)
            one.start()
            sent.append(one)

        def arrived(slot, h, i):
            part(slot, h, i, sib).wait_recv()

        go(M, 0, 2, right)
        go(M, 1, 5, left)
        go(M, 0, 0, sib)
        go(M, 1, 1, sib)
        go(M, 1, 3, right)
        go(M, 0, 4, left)
        use(M, True)
        arrived(left, 0, 2)
        go(left, 0, 6, right)
        go(left, 0, 8, sib)
        arrived(right, 1, 5)
        go(right, 1, 7, left)
        go(right, 1, 11, sib)
        arrived(sib, 0, 0)
        arrived(sib, 1, 1)
        use(sib, False)
        arrived(left, 1, 3)
        go(left, 1, 9, sib)
        arrived(right, 0, 4)
        go(right, 0, 10, sib)
        use(left, False)
        use(right, False)
        arrived(opp, 0, 6)
        go(opp, 0, 12, sib)
        arrived(opp, 1, 7)
        go(opp, 1, 13, sib)
        use(opp, False)
        for yy, i in ((left_y, 8), (right_y, 10), (opp_y, 12)):
            slot = 2 * yy + 1 - core
            arrived(slot, 0, i)
            arrived(slot, 1, i + 1)
            use(slot, False)
        return sent

    wait_bytes(w_v, w_sem)

    def project(m, first):
        term = dot(feat[m], w_v[m].reshape(256, 640))
        proj[...] = term if first else proj[...] + term

    pending = gather(feat, f_send, f_recv, project)

    bias_row, gain_row = bias_v[...], gain_v[...]
    mine_c, mine_k = T // 8, lax.rem(T, 8)

    @pl.loop(0, CH)
    def _(i):
        c = lax.rem(mine_c + i, CH)
        rows = pl.ds(pl.multiple_of(c * FR, FR), FR)
        logit = proj[rows, 384:512] + bias_row
        u = jnp.exp(-jnp.abs(logit))
        log1p = jnp.where(u < 1e-3, u * (1.0 - 0.5 * u), jnp.log(1.0 + u))
        log_decay = jnp.minimum(logit, 0.0) - log1p
        both = dot(tri, jnp.concatenate(split(log_decay), 1))
        total = both[:, :128] + both[:, 128:]
        decay_log[rows, :] = total
        seen = rcol[c]
        last, last_seen = total[FR - 1 :], seen[FR - 1 :]
        weight = jnp.where(seen == last_seen, jnp.exp(jnp.minimum(last - total, 0.0)), 0.0)
        state = dot3(proj[rows, 128:256] * weight, proj[rows, 256:384], ((0,), (0,)))
        sbuf[pl.ds(pl.multiple_of(c * 8, 8), 8)] = state.astype(BF).reshape(8, 16, 128)
        dbuf[c] = jnp.where(last_seen == 0.0, jnp.exp(last), 0.0)

        @pl.loop(0, 8)
        def _(n):
            peer = c * 8 + lax.rem(mine_k + n, 8)

            @pl.when(peer != T)
            def _():
                piece(dbuf.at[c], d_in.at[T], dk_sem, peer).start()
                piece(sbuf.at[peer], st_in.at[T], st_sem, peer).start()

    d_in[T] = dbuf[mine_c]
    st_in[T] = sbuf[T]

    @pl.loop(0, CH)
    def _(c):
        rows = pl.ds(pl.multiple_of(c * FR, FR), FR)
        total = decay_log[rows, :]
        queries = proj[rows, 0:128] * HK ** (-0.5)
        keys, values = proj[rows, 128:256], proj[rows, 256:384]
        seen = rcol[c]
        carried_q[rows, :] = jnp.where(seen == 0.0, queries * jnp.exp(total), 0.0)
        picked = dot(sel[...], jnp.concatenate(split(total), 1))
        picked = picked[:, :128] + picked[:, 128:]
        scores = masks[len(LEVELS)] * dot3(queries, keys, ((1,), (1,)))
        for i in range(len(LEVELS)):
            gap = jnp.exp(-jnp.abs(total - picked[i * FR : (i + 1) * FR]))
            scores += masks[i] * dot3(queries * gap, keys * gap, ((1,), (1,)))
        scores = jnp.where(seen[:, :FR] == rrow[c], scores, 0.0)
        attended[rows, :] = dot3(scores, values)
        gate = proj[rows, 512:640]
        silu[rows, :] = gate / (1.0 + jnp.exp(-gate))

    wait_bytes(d_in.at[pl.ds(0, TM - 1)], dk_sem.at[1])
    wait_bytes(st_in.at[pl.ds(0, TM - 1)], st_sem.at[1])
    d_t[...] = d_in[...].reshape(TM, 128).T
    decays = d_t[pl.ds(pl.multiple_of(mine_k * 16, 16), 16), :]
    state = jnp.zeros((16, 128), F32)
    for t in range(TM):
        pre[t] = state.astype(BF)
        if t < TM - 1:
            state = state * decays[:, t : t + 1] + st_in[t].astype(F32)

    @pl.loop(1, TM)
    def _(k):
        peer = lax.rem(T + k, TM)
        piece(pre.at[peer], s_in.at[T], p_sem, peer).start()

    s_in[T] = pre[T]
    wait_bytes(s_in.at[pl.ds(0, TM - 1)], p_sem.at[1])

    @pl.loop(0, CH)
    def _(c):
        rows = pl.ds(pl.multiple_of(c * FR, FR), FR)
        entering = s_in[pl.ds(pl.multiple_of(c * 8, 8), 8)].reshape(128, 128)
        q2 = jnp.concatenate(split(carried_q[rows, :]), 1)
        full = attended[rows, :] + dot(q2, jnp.concatenate([entering, entering], 0))
        square = jnp.mean(full * full, axis=-1, keepdims=True)
        attended[rows, :] = full * lax.rsqrt(square + 1e-06) * gain_row

    normed = attended[...]
    mixed = dot(mix[...], jnp.concatenate(split(normed), 1))
    blended = normed + (mixed[:, :128] + mixed[:, 128:]) * inv_partners[...]
    gat[M] = (blended * silu[...]).astype(BF)

    def produce(m, first):
        rows = gat[m]
        term = dot(rows, ow_v[m])
        oacc[...] = term if first else oacc[...] + term
        part = dot(rows, cot_v[...], ((0,), (0,))).reshape(8, 16, 256)
        gradf[m] = part
        gbuf[m] = part.astype(BF)

    pending += gather(gat, g_send, g_recv, produce)

    def along_x(d):
        to = lax.rem(x + d, NX)
        return piece(gbuf.at[pl.ds(2 * to, 2)], xr.at[x], x_sem, to * NZ + z)

    across = [along_x(d) for d in (2, 1, 3)]
    for one in across:
        one.start()
    out_v[...] = oacc[...].astype(BF)
    store = pltpu.make_async_copy(out_v, out, out_sem.at[0])
    store.start()

    wait_bytes(xr.at[pl.ds(0, NX - 1)], x_sem.at[1])
    total = gradf[pl.ds(2 * x, 2)]
    for d in range(1, NX):
        total += xr[lax.rem(x + d, NX)].astype(F32)
    total = total.reshape(NZ, 16, 256)
    zf[...] = total
    zbuf[...] = total.astype(BF)

    @pl.loop(1, NZ)
    def _(k):
        to = lax.rem(z + k, NZ)
        piece(zbuf.at[to], zr.at[z], z_sem, x * NZ + to).start()

    wait_bytes(zr.at[pl.ds(0, NZ - 1)], z_sem.at[1])
    total = zf[z]
    for k in range(1, NZ):
        total += zr[lax.rem(z + k, NZ)].astype(F32)
    grad_v[...] = total
    last_store = pltpu.make_async_copy(grad_v, grad, out_sem.at[1])
    last_store.start()

    wait_bytes(pack.at[pl.ds(0, TM - 1)], a_sem.at[0])
    for one in pending:
        one.wait_send()
    wait_bytes(d_in.at[pl.ds(0, TM - 1)], dk_sem.at[0])
    wait_bytes(sbuf.at[pl.ds(0, TM - 1)], st_sem.at[0])
    wait_bytes(pre.at[pl.ds(0, TM - 1)], p_sem.at[0])
    wait_bytes(xr.at[pl.ds(0, NX - 1)], x_sem.at[0])
    wait_bytes(zbuf.at[pl.ds(0, NZ - 1)], z_sem.at[0])
    store.wait()
    last_store.wait()


def local(
    observations, contact, resets, q_weight, k_weight, v_weight, decay_weight, gate_weight,
    decay_bias, norm_gain, out_weight, out_cotangent,
):
    features = jnp.swapaxes(observations[0], 0, 1)
    weights = [
        w.reshape(8, MP, 2, 16, 128) for w in (q_weight, k_weight, v_weight, decay_weight, gate_weight)
    ]
    vm = pltpu.VMEM
    dma = pltpu.SemaphoreType.DMA
    scratch = [
        vm((32, 4096), BF), vm((FR, CH), jnp.int32), vm((CH, FR), jnp.int32),
        vm((MP, 2, 8, 16, 640), BF), vm((1, 128), F32), vm((1, 128), F32),
        vm((MP, 128, 256), BF), vm((ROWS, 256), BF),
        vm((TM, 16, 128), BF), vm((TM, 16, 128), BF), vm((MP, ROWS, 256), BF),
        vm((ROWS, 640), F32), vm((ROWS, 128), F32), vm((CH, FR, 128), F32), vm((CH, 1, FR), F32),
        vm((len(LEVELS) + 1, FR, FR), F32), vm((len(LEVELS) * FR, FR), BF),
        vm((ROWS, ROWS), BF), vm((ROWS, 128), F32),
        vm((TM, 16, 128), BF), vm((CH, 1, 128), F32), vm((TM, 16, 128), BF), vm((TM, 1, 128), F32),
        vm((128, TM), F32), vm((TM, 16, 128), BF), vm((TM, 16, 128), BF),
        vm((ROWS, 128), F32), vm((ROWS, 128), F32), vm((ROWS, 128), F32),
        vm((MP, ROWS, 128), BF), vm((ROWS, 256), F32), vm((MP, 8, 16, 256), F32),
        vm((MP, 8, 16, 256), BF), vm((NX, 2, 8, 16, 256), BF), vm((NZ, 16, 256), F32),
        vm((NZ, 16, 256), BF), vm((NZ, 16, 256), BF), vm((ROWS, 256), BF), vm((16, 256), F32),
        dma((7,)), dma, dma((2,)), dma((2,)), dma((14,)), dma((14,)), dma((2,)), dma((2,)), dma((2,)),
        dma((14,)), dma((14,)), dma((2,)), dma((2,)),
    ]
    following, weight_grad = pl.pallas_call(
        kernel,
        out_shape=(
            jax.ShapeDtypeStruct((ROWS, 256), BF),
            jax.ShapeDtypeStruct((16, 256), F32),
        ),
        in_specs=[pl.BlockSpec(memory_space=pl.ANY)] * 12,
        out_specs=(pl.BlockSpec(memory_space=pl.ANY),) * 2,
        scratch_shapes=scratch,
        compiler_params=pltpu.CompilerParams(
            collective_id=0, has_side_effects=True, vmem_limit_bytes=40 * 2**20
        ),
    )(
        features, contact.reshape(FR, CH), resets, *weights, decay_bias, norm_gain,
        out_weight.reshape(MP, 128, 256), out_cotangent.reshape(ROWS, 256),
    )
    return following.reshape(CH, FR, 256), weight_grad


def solution(mesh):
    placed = (
        P("tm", None, "mp"),
        P("tm", None, None),
        P(None, "tm"),
        P(None, "mp"),
        P(None, "mp"),
        P(None, "mp"),
        P(None, "mp"),
        P(None, "mp"),
        P("mp", None),
        P("mp", None),
        P(None, "mp"),
        P(None, "tm", "mp"),
    )
    return jax.shard_map(
        local,
        mesh=mesh,
        in_specs=placed,
        out_specs=(P(None, "tm", "mp"), P("tm", "mp")),
        check_vma=False,
    )
```

```python
import jax
import jax.numpy as jnp
from jax import lax
from jax.experimental import pallas as pl
from jax.experimental.pallas import tpu as pltpu
from jax.sharding import PartitionSpec as P

MESH = pl.DeviceIdType.MESH
BF = jnp.bfloat16
F32 = jnp.float32

HK = 128
CH = 8
TM, MP = 64, 8
NX, NZ, NY = 4, 16, 4
FR = 64
ROWS = CH * FR
LEVELS = (32, 16, 8, 4, 2, 1)


def dot(a, b, dims=((1,), (0,))):
    return lax.dot_general(a, b, (dims, ((), ())), preferred_element_type=F32)


def split(a):
    high = a.astype(BF)
    return high, (a - high.astype(F32)).astype(BF)


def dot3(a, b, dims=((1,), (0,))):
    ah, al = split(a)
    bh, bl = split(b)
    da, db = dims[0][0], dims[1][0]
    return dot(jnp.concatenate([ah, al, ah], da), jnp.concatenate([bh, bh, bl], db), dims)


def iota(shape, dim):
    return lax.broadcasted_iota(jnp.int32, shape, dim)


def kernel(
    obs, contact, resets, wq, wk, wv, wd, wg, bias, gain, ow, cot,
    out, grad,
    obs_v, con_v, res_v, w_v, bias_v, gain_v, ow_v, cot_v,
    pack, rx, feat, proj, decay_log, rcol, rrow, masks, sel, mix, inv_partners,
    sbuf, dbuf, st_in, d_in, d_t, pre, s_in, attended, carried_q, silu,
    gat, oacc, gradf, gbuf, xr, zf, zbuf, zr, out_v, grad_v,
    in_sem, w_sem, out_sem, a_send, a_recv, f_send, f_recv, st_sem, dk_sem, p_send, p_recv, g_send, g_recv, x_sem, z_sem,
):
    T = lax.axis_index("tm")
    M = lax.axis_index("mp")
    x, z = T // NZ, lax.rem(T, NZ)
    y, core = M // 2, lax.rem(M, 2)
    right_y, left_y, opp_y = lax.rem(y + 1, NY), lax.rem(y + 3, NY), lax.rem(y + 2, NY)

    def load(src, dst, i):
        return pltpu.make_async_copy(src, dst, in_sem.at[i])

    loads = [
        load(obs, obs_v, 0), load(contact, con_v, 1), load(resets, res_v, 2), load(bias, bias_v, 3),
        load(gain, gain_v, 4), load(ow, ow_v, 5), load(cot, cot_v, 6),
    ]
    loads[0].start()

    barrier = pltpu.get_barrier_semaphore()

    @pl.loop(1, TM)
    def _(k):
        pl.semaphore_signal(barrier, inc=1, device_id=(lax.rem(T + k, TM), M), device_id_type=MESH)

    sib = 2 * y + 1 - core
    right, left, opp = 2 * right_y + core, 2 * left_y + core, 2 * opp_y + core
    for other in (sib, right, left):
        pl.semaphore_signal(barrier, inc=1, device_id=(T, other), device_id_type=MESH)

    for one in loads[1:]:
        one.start()

    @pl.loop(0, MP)
    def _(m):
        for j, w in enumerate((wq, wk, wv, wd, wg)):
            for fh in range(2):
                pltpu.make_async_copy(
                    w.at[:, m, fh], w_v.at[m, fh, :, :, pl.ds(j * 128, 128)], w_sem
                ).start()

    loads[0].wait()
    low = iota((16, 128), 1) < 64

    @pl.loop(0, TM // 2)
    def _(u):
        tile = obs_v[:, pl.ds(pl.multiple_of(u * 128, 128), 128)].astype(F32)
        a, b = tile[:16], tile[16:]
        pack[2 * u] = jnp.where(low, a, pltpu.roll(b, 64, 1)).astype(BF)
        pack[2 * u + 1] = jnp.where(low, pltpu.roll(a, 64, 1), b).astype(BF)

    pl.semaphore_wait(barrier, TM - 1 + 3)

    def piece(src, dst, sems, peer):
        return pltpu.make_async_remote_copy(
            src_ref=src, dst_ref=dst, send_sem=sems.at[0], recv_sem=sems.at[1],
            device_id=(peer, M), device_id_type=MESH,
        )

    def wait_bytes(ref, sem):
        pltpu.make_async_copy(ref, ref, sem).wait()

    def piece_of_wave(src, dst, send, recv, d, peer):
        return pltpu.make_async_remote_copy(
            src_ref=src, dst_ref=dst, send_sem=send, recv_sem=recv.at[d],
            device_id=(peer, M), device_id_type=MESH,
        )

    def to_wave(src, dst, send, recv, d):
        @pl.loop(1 if d == 0 else 0, NZ)
        def _(k):
            peer = lax.rem(x + d, NX) * NZ + lax.rem(z + k, NZ)
            piece_of_wave(src.at[peer], dst.at[T], send, recv, d, peer).start()

    def from_wave(dst, recv, d):
        wait_bytes(dst.at[pl.ds(0, NZ - 1 if d == 0 else NZ)], recv.at[d])

    source = [lax.rem(x + NX - d, NX) for d in range(NX)]

    for d in range(NX):
        to_wave(pack, rx, a_send, a_recv, d)

    rx[T] = pack[T]

    for one in loads[1:]:
        one.wait()
    tri = (iota((FR, FR), 0) >= iota((FR, FR), 1)).astype(BF)
    res = res_v[...].astype(F32).astype(BF)
    seen_col = dot(tri, res, ((1,), (1,)))
    seen_row = dot(res, tri, ((1,), (1,)))
    for c in range(CH):
        rcol[c] = jnp.broadcast_to(seen_col[:, c : c + 1], (FR, 128))
        rrow[c] = seen_row[c : c + 1, :]
    t_id, s_id = iota((FR, FR), 0), iota((FR, FR), 1)
    for i, h in enumerate(LEVELS):
        masks[i] = ((t_id // (2 * h) == s_id // (2 * h)) & (t_id // h > s_id // h)).astype(F32)
        sel[i * FR : (i + 1) * FR] = (s_id == (t_id // (2 * h)) * (2 * h) + h - 1).astype(BF)
    masks[len(LEVELS)] = (t_id == s_id).astype(F32)

    row_q, col_q = iota((ROWS, FR), 0), iota((ROWS, FR), 1)
    pick = (((row_q % FR) // 8) * 8 + row_q // FR == col_q).astype(BF)
    con = con_v[...].astype(F32).astype(BF)
    taken = dot(pick, con).astype(BF)
    inv_partners[...] = 1.0 / jnp.maximum(dot(taken, jnp.ones((CH, 128), BF)), 1.0)
    spread = (iota((CH, ROWS), 1) // FR == iota((CH, ROWS), 0)).astype(BF)
    same = iota((ROWS, ROWS), 0) % FR == iota((ROWS, ROWS), 1) % FR
    mix[...] = jnp.where(same, dot(taken, spread), 0.0).astype(BF)

    wait_bytes(w_v, w_sem)
    bias_row, gain_row = bias_v[...], gain_v[...]
    mine_c, mine_k = T // 8, lax.rem(T, 8)
    pending = []

    def send(one):
        one.start()
        pending.append(one)

    def wave_rows(d):
        return pl.ds(pl.multiple_of(source[d] * 2 * FR, 2 * FR), 2 * FR)

    def part(d, slot, i, to):
        ref = feat.at[slot, wave_rows(d)]
        return pltpu.make_async_remote_copy(
            src_ref=ref, dst_ref=ref, send_sem=f_send.at[d, i], recv_sem=f_recv.at[d, i],
            device_id=(T, to), device_id_type=MESH,
        )

    def own_features(d):
        from_wave(rx, a_recv, d)
        for c in range(2):
            tiles = rx[pl.ds(pl.multiple_of(source[d] * NZ + c * 8, 8), 8)]
            turned = tiles.reshape(128, 128).T
            rows = pl.ds(pl.multiple_of((source[d] * 2 + c) * FR, FR), FR)
            feat[M, rows, 0:128] = turned[:FR]
            feat[M, rows, 128:256] = turned[FR:]
        send(part(d, M, 1, right))
        send(part(d, M, 2, left))
        send(part(d, M, 0, sib))

    def pass_on(d):
        for slot, i, to in ((left, 1, right), (right, 2, left)) if d % 2 == 0 else ((right, 2, left), (left, 1, right)):
            part(d, slot, i, sib).wait_recv()
            if (i == 1) == (d % 2 == 0):
                send(part(d, slot, 3, to))
            send(part(d, slot, 3 + i, sib))

    def pass_opposite(d):
        part(d, opp, 3, sib).wait_recv()
        send(part(d, opp, 6, sib))

    def add_projections(d, slots, first):
        rows = wave_rows(d)
        total = None if first else proj[rows, :]
        for slot in slots:
            term = dot(feat[slot, rows], w_v[slot].reshape(256, 640))
            total = term if total is None else total + term
        proj[rows, :] = total

    def project(d):
        part(d, sib, 0, sib).wait_recv()
        add_projections(d, (M, left, right, opp, sib), True)
        others = [2 * yy + 1 - core for yy in (left_y, right_y, opp_y)]
        for slot, i in zip(others, (4, 5, 6)):
            part(d, slot, i, sib).wait_recv()
        add_projections(d, others, False)

    def states(d):
        for n in range(2):
            c = source[d] * 2 + n
            rows = pl.ds(pl.multiple_of(c * FR, FR), FR)
            logit = proj[rows, 384:512] + bias_row
            u = jnp.exp(-jnp.abs(logit))
            log1p = jnp.where(u < 1e-3, u * (1.0 - 0.5 * u), jnp.log(1.0 + u))
            log_decay = jnp.minimum(logit, 0.0) - log1p
            both = dot(tri, jnp.concatenate(split(log_decay), 1))
            total = both[:, :128] + both[:, 128:]
            decay_log[rows, :] = total
            seen = rcol[c]
            last, last_seen = total[FR - 1 :], seen[FR - 1 :]
            weight = jnp.where(seen == last_seen, jnp.exp(jnp.minimum(last - total, 0.0)), 0.0)
            state = dot3(proj[rows, 128:256] * weight, proj[rows, 256:384], ((0,), (0,)))
            sbuf[pl.ds(pl.multiple_of(c * 8, 8), 8)] = state.astype(BF).reshape(8, 16, 128)
            dbuf[c] = jnp.where(last_seen == 0.0, jnp.exp(last), 0.0)

        @pl.loop(1 if d == 0 else 0, NZ)
        def _(k):
            to = lax.rem(z + k, NZ)
            peer = source[d] * NZ + to
            piece(dbuf.at[source[d] * 2 + to // 8], d_in.at[T], dk_sem, peer).start()
            piece(sbuf.at[peer], st_in.at[T], st_sem, peer).start()

    own_features(0)
    own_features(1)
    pass_on(0)
    pass_opposite(0)
    project(0)
    states(0)
    own_features(2)
    pass_on(1)
    pass_opposite(1)
    project(1)
    states(1)
    own_features(3)
    pass_on(2)
    pass_opposite(2)
    pass_on(3)
    project(2)
    states(2)
    pass_opposite(3)
    project(3)
    states(3)
    d_in[T] = dbuf[mine_c]
    st_in[T] = sbuf[T]

    @pl.loop(0, CH)
    def _(c):
        rows = pl.ds(pl.multiple_of(c * FR, FR), FR)
        total = decay_log[rows, :]
        queries = proj[rows, 0:128] * HK ** (-0.5)
        keys, values = proj[rows, 128:256], proj[rows, 256:384]
        seen = rcol[c]
        carried_q[rows, :] = jnp.where(seen == 0.0, queries * jnp.exp(total), 0.0)
        picked = dot(sel[...], jnp.concatenate(split(total), 1))
        picked = picked[:, :128] + picked[:, 128:]
        scores = masks[len(LEVELS)] * dot3(queries, keys, ((1,), (1,)))
        for i in range(len(LEVELS)):
            gap = jnp.exp(-jnp.abs(total - picked[i * FR : (i + 1) * FR]))
            scores += masks[i] * dot3(queries * gap, keys * gap, ((1,), (1,)))
        scores = jnp.where(seen[:, :FR] == rrow[c], scores, 0.0)
        attended[rows, :] = dot3(scores, values)
        gate = proj[rows, 512:640]
        silu[rows, :] = gate / (1.0 + jnp.exp(-gate))

    wait_bytes(d_in.at[pl.ds(0, TM - 1)], dk_sem.at[1])
    wait_bytes(st_in.at[pl.ds(0, TM - 1)], st_sem.at[1])
    d_t[...] = d_in[...].reshape(TM, 128).T
    decays = d_t[pl.ds(pl.multiple_of(mine_k * 16, 16), 16), :]
    state = jnp.zeros((16, 128), F32)
    for t in range(TM):
        pre[t] = state.astype(BF)
        if t < TM - 1:
            state = state * decays[:, t : t + 1] + st_in[t].astype(F32)

    for d in range(NX):
        to_wave(pre, s_in, p_send, p_recv, d)

    s_in[T] = pre[T]
    for d in range(NX):
        from_wave(s_in, p_recv, d)
        for n in range(2):
            c = source[d] * 2 + n
            rows = pl.ds(pl.multiple_of(c * FR, FR), FR)
            entering = s_in[pl.ds(pl.multiple_of(c * 8, 8), 8)].reshape(128, 128)
            q2 = jnp.concatenate(split(carried_q[rows, :]), 1)
            full = attended[rows, :] + dot(q2, jnp.concatenate([entering, entering], 0))
            square = jnp.mean(full * full, axis=-1, keepdims=True)
            attended[rows, :] = full * lax.rsqrt(square + 1e-06) * gain_row

    normed = attended[...]
    mixed = dot(mix[...], jnp.concatenate(split(normed), 1))
    blended = normed + (mixed[:, :128] + mixed[:, 128:]) * inv_partners[...]
    gat[M] = (blended * silu[...]).astype(BF)

    half = ROWS // 2

    def gated_part(slot, h, i, to):
        ref = gat.at[slot, pl.ds(h * half, half)]
        return pltpu.make_async_remote_copy(
            src_ref=ref, dst_ref=ref, send_sem=g_send.at[i], recv_sem=g_recv.at[i],
            device_id=(T, to), device_id_type=MESH,
        )

    def go(*args):
        send(gated_part(*args))

    def arrived(slot, h, i):
        gated_part(slot, h, i, sib).wait_recv()

    def produce(m, first=False):
        rows = gat[m]
        term = dot(rows, ow_v[m])
        oacc[...] = term if first else oacc[...] + term
        part = dot(rows, cot_v[...], ((0,), (0,))).reshape(8, 16, 256)
        gradf[m] = part
        gbuf[m] = part.astype(BF)

    def along_x(to):
        @pl.when(to != x)
        def _():
            piece(gbuf.at[pl.ds(2 * to, 2)], xr.at[x], x_sem, to * NZ + z).start()

    go(M, 0, 2, right)
    go(M, 1, 5, left)
    go(M, 0, 0, sib)
    go(M, 1, 1, sib)
    go(M, 1, 3, right)
    go(M, 0, 4, left)
    produce(M, True)
    arrived(left, 0, 2)
    go(left, 0, 6, right)
    go(left, 0, 8, sib)
    arrived(right, 1, 5)
    go(right, 1, 7, left)
    go(right, 1, 11, sib)
    arrived(sib, 0, 0)
    arrived(sib, 1, 1)
    produce(sib)
    along_x(y)
    arrived(left, 1, 3)
    go(left, 1, 9, sib)
    arrived(right, 0, 4)
    go(right, 0, 10, sib)
    produce(left)
    arrived(opp, 0, 6)
    go(opp, 0, 12, sib)
    arrived(opp, 1, 7)
    go(opp, 1, 13, sib)
    produce(right)
    for yy, i in ((left_y, 8), (right_y, 10), (opp_y, 12)):
        slot = 2 * yy + 1 - core
        arrived(slot, 0, i)
        arrived(slot, 1, i + 1)
        if i == 12:
            produce(opp)
        produce(slot)
        along_x(yy)

    out_v[...] = oacc[...].astype(BF)
    store = pltpu.make_async_copy(out_v, out, out_sem.at[0])
    store.start()

    wait_bytes(xr.at[pl.ds(0, NX - 1)], x_sem.at[1])
    total = gradf[pl.ds(2 * x, 2)]
    for d in range(1, NX):
        total += xr[lax.rem(x + d, NX)].astype(F32)
    total = total.reshape(NZ, 16, 256)
    zf[...] = total
    zbuf[...] = total.astype(BF)

    @pl.loop(1, NZ)
    def _(k):
        to = lax.rem(z + k, NZ)
        piece(zbuf.at[to], zr.at[z], z_sem, x * NZ + to).start()

    wait_bytes(zr.at[pl.ds(0, NZ - 1)], z_sem.at[1])
    total = zf[z]
    for k in range(1, NZ):
        total += zr[lax.rem(z + k, NZ)].astype(F32)
    grad_v[...] = total
    last_store = pltpu.make_async_copy(grad_v, grad, out_sem.at[1])
    last_store.start()

    wait_bytes(pack.at[pl.ds(0, TM - 1)], a_send)
    for one in pending:
        one.wait_send()
    wait_bytes(d_in.at[pl.ds(0, TM - 1)], dk_sem.at[0])
    wait_bytes(sbuf.at[pl.ds(0, TM - 1)], st_sem.at[0])
    wait_bytes(pre.at[pl.ds(0, TM - 1)], p_send)
    wait_bytes(xr.at[pl.ds(0, NX - 1)], x_sem.at[0])
    wait_bytes(zbuf.at[pl.ds(0, NZ - 1)], z_sem.at[0])
    store.wait()
    last_store.wait()


def local(
    observations, contact, resets, q_weight, k_weight, v_weight, decay_weight, gate_weight,
    decay_bias, norm_gain, out_weight, out_cotangent,
):
    features = jnp.swapaxes(observations[0], 0, 1)
    weights = [
        w.reshape(8, MP, 2, 16, 128) for w in (q_weight, k_weight, v_weight, decay_weight, gate_weight)
    ]
    vm = pltpu.VMEM
    dma = pltpu.SemaphoreType.DMA
    scratch = [
        vm((32, 4096), BF), vm((FR, CH), jnp.int32), vm((CH, FR), jnp.int32),
        vm((MP, 2, 8, 16, 640), BF), vm((1, 128), F32), vm((1, 128), F32),
        vm((MP, 128, 256), BF), vm((ROWS, 256), BF),
        vm((TM, 16, 128), BF), vm((TM, 16, 128), BF), vm((MP, ROWS, 256), BF),
        vm((ROWS, 640), F32), vm((ROWS, 128), F32), vm((CH, FR, 128), F32), vm((CH, 1, FR), F32),
        vm((len(LEVELS) + 1, FR, FR), F32), vm((len(LEVELS) * FR, FR), BF),
        vm((ROWS, ROWS), BF), vm((ROWS, 128), F32),
        vm((TM, 16, 128), BF), vm((CH, 1, 128), F32), vm((TM, 16, 128), BF), vm((TM, 1, 128), F32),
        vm((128, TM), F32), vm((TM, 16, 128), BF), vm((TM, 16, 128), BF),
        vm((ROWS, 128), F32), vm((ROWS, 128), F32), vm((ROWS, 128), F32),
        vm((MP, ROWS, 128), BF), vm((ROWS, 256), F32), vm((MP, 8, 16, 256), F32),
        vm((MP, 8, 16, 256), BF), vm((NX, 2, 8, 16, 256), BF), vm((NZ, 16, 256), F32),
        vm((NZ, 16, 256), BF), vm((NZ, 16, 256), BF), vm((ROWS, 256), BF), vm((16, 256), F32),
        dma((7,)), dma, dma((2,)), dma, dma((NX,)), dma((NX, 7)), dma((NX, 7)), dma((2,)), dma((2,)), dma, dma((NX,)),
        dma((14,)), dma((14,)), dma((2,)), dma((2,)),
    ]
    following, weight_grad = pl.pallas_call(
        kernel,
        out_shape=(
            jax.ShapeDtypeStruct((ROWS, 256), BF),
            jax.ShapeDtypeStruct((16, 256), F32),
        ),
        in_specs=[pl.BlockSpec(memory_space=pltpu.HBM)] * 12,
        out_specs=(pl.BlockSpec(memory_space=pltpu.HBM),) * 2,
        scratch_shapes=scratch,
        compiler_params=pltpu.CompilerParams(
            collective_id=0, has_side_effects=True, vmem_limit_bytes=60 * 2**20
        ),
    )(
        features, contact.reshape(FR, CH), resets, *weights, decay_bias, norm_gain,
        out_weight.reshape(MP, 128, 256), out_cotangent.reshape(ROWS, 256),
    )
    return following.reshape(CH, FR, 256), weight_grad


def solution(mesh):
    placed = (
        P("tm", None, "mp"),
        P("tm", None, None),
        P(None, "tm"),
        P(None, "mp"),
        P(None, "mp"),
        P(None, "mp"),
        P(None, "mp"),
        P(None, "mp"),
        P("mp", None),
        P("mp", None),
        P(None, "mp"),
        P(None, "tm", "mp"),
    )
    return jax.shard_map(
        local,
        mesh=mesh,
        in_specs=placed,
        out_specs=(P(None, "tm", "mp"), P("tm", "mp")),
        check_vma=False,
    )
```

```python
import jax
import jax.numpy as jnp
from jax import lax
from jax.experimental import pallas as pl
from jax.experimental.pallas import tpu as pltpu
from jax.sharding import PartitionSpec as P

MESH = pl.DeviceIdType.MESH
BF = jnp.bfloat16
F32 = jnp.float32

HK = 128
CH = 8
TM, MP = 64, 8
NX, NZ, NY = 4, 16, 4
FR = 64
ROWS = CH * FR
LEVELS = (32, 16, 8, 4, 2, 1)
WAVE = 2 * FR


def dot(a, b, dims=((1,), (0,))):
    return lax.dot_general(a, b, (dims, ((), ())), preferred_element_type=F32)


def split(a):
    high = a.astype(BF)
    return high, (a - high.astype(F32)).astype(BF)


def dot3(a, b, dims=((1,), (0,))):
    ah, al = split(a)
    bh, bl = split(b)
    da, db = dims[0][0], dims[1][0]
    return dot(jnp.concatenate([ah, al, ah], da), jnp.concatenate([bh, bh, bl], db), dims)


def iota(shape, dim):
    return lax.broadcasted_iota(jnp.int32, shape, dim)


def column(row):
    return jnp.broadcast_to(row, (8, 128)).T[:, :1]


def kernel(
    obs, contact, resets, wq, wk, wv, wd, wg, bias, gain, ow, cot,
    out, grad,
    con_v, res_v, w_v, bias_v, gain_v, ow_v, cot_v,
    rx, feat, proj, decay_log, res_own, res_in, rcol, rrow, masks, sel, mix, inv_partners,
    local_state, before, s_own, d_own, s_in, d_in, attended, carried_q,
    gate_own, gate_in, norm_own, norm_in,
    gat, oacc, gradf, gbuf, xr, zf, zbuf, zr, out_v, grad_v,
    in_sem, w_sem, out_sem, a_send, a_recv, f_send, f_recv, r_sem, s_send, s_recv, d_send, d_recv,
    gate_sem, norm_sem, g_send, g_recv, x_sem, z_sem,
):
    T = lax.axis_index("tm")
    M = lax.axis_index("mp")
    x, z = T // NZ, lax.rem(T, NZ)
    y, core = M // 2, lax.rem(M, 2)
    span, place = T // CH, lax.rem(T, CH)
    char = lax.rem(place + span, CH)

    def holder(other_span, other_char):
        return other_span * CH + lax.rem(other_char - other_span + CH, CH)

    right_y, left_y, opp_y = lax.rem(y + 1, NY), lax.rem(y + 3, NY), lax.rem(y + 2, NY)

    def load(src, dst, i):
        return pltpu.make_async_copy(src, dst, in_sem.at[i])

    loads = [
        load(resets, res_v, 0), load(contact, con_v, 1), load(bias, bias_v, 2),
        load(gain, gain_v, 3), load(ow, ow_v, 4), load(cot, cot_v, 5),
    ]
    loads[0].start()

    barrier = pltpu.get_barrier_semaphore()

    @pl.loop(1, TM)
    def _(k):
        pl.semaphore_signal(barrier, inc=1, device_id=(lax.rem(T + k, TM), M), device_id_type=MESH)

    sib = 2 * y + 1 - core
    right, left, opp = 2 * right_y + core, 2 * left_y + core, 2 * opp_y + core
    for other in (sib, right, left):
        pl.semaphore_signal(barrier, inc=1, device_id=(T, other), device_id_type=MESH)

    for one in loads[1:]:
        one.start()

    @pl.loop(0, MP)
    def _(m):
        for j, w in enumerate((wq, wk, wv, wd, wg)):
            pltpu.make_async_copy(w.at[:, m], w_v.at[m, :, :, pl.ds(j * 128, 128)], w_sem).start()

    loads[0].wait()
    res = res_v[...].astype(F32)
    res = jnp.concatenate([res, jnp.zeros_like(res)], 1)
    for c in range(CH):
        res_own[c] = res[c : c + 1]
    res_in[place] = res_own[char]

    pl.semaphore_wait(barrier, TM - 1 + 3)

    def piece(src, dst, sems, peer):
        return pltpu.make_async_remote_copy(
            src_ref=src, dst_ref=dst, send_sem=sems.at[0], recv_sem=sems.at[1],
            device_id=(peer, M), device_id_type=MESH,
        )

    def wait_bytes(ref, sem):
        pltpu.make_async_copy(ref, ref, sem).wait()

    def piece_of_wave(src, dst, send, recv, d, peer):
        return pltpu.make_async_remote_copy(
            src_ref=src, dst_ref=dst, send_sem=send, recv_sem=recv.at[d],
            device_id=(peer, M), device_id_type=MESH,
        )

    def quarter(to, d):
        return obs.at[:, pl.ds(pl.multiple_of(to * CH * FR + d * WAVE, WAVE), WAVE)]

    for d in range(NX):
        @pl.loop(0, CH)
        def _(k):
            to = lax.rem(span + k, CH)
            peer = holder(to, span)

            @pl.when(peer != T)
            def _():
                pltpu.make_async_remote_copy(
                    src_ref=quarter(to, d), dst_ref=rx.at[d, place], send_sem=a_send, recv_sem=a_recv.at[d],
                    device_id=(peer, M), device_id_type=MESH,
                ).start()

        @pl.when(place == 0)
        def _():
            pltpu.make_async_copy(quarter(span, d), rx.at[d, place], a_recv.at[d]).start()

    @pl.loop(1, CH)
    def _(k):
        to = lax.rem(place + k, CH)
        piece(res_own.at[lax.rem(to + span, CH)], res_in.at[place], r_sem, span * CH + to).start()

    for one in loads[1:]:
        one.wait()
    tri = (iota((FR, FR), 0) >= iota((FR, FR), 1)).astype(BF)
    wait_bytes(res_in.at[pl.ds(0, CH - 1)], r_sem.at[1])
    res = res_in[...].reshape(CH, 128)[:, :FR].astype(BF)
    seen_col = dot(tri, res, ((1,), (1,)))
    seen_row = dot(res, tri, ((1,), (1,)))
    for c in range(CH):
        rcol[c] = jnp.broadcast_to(seen_col[:, c : c + 1], (FR, 128))
        rrow[c] = seen_row[c : c + 1, :]
    t_id, s_id = iota((FR, FR), 0), iota((FR, FR), 1)
    for i, h in enumerate(LEVELS):
        masks[i] = ((t_id // (2 * h) == s_id // (2 * h)) & (t_id // h > s_id // h)).astype(F32)
        sel[i * FR : (i + 1) * FR] = (s_id == (t_id // (2 * h)) * (2 * h) + h - 1).astype(BF)
    masks[len(LEVELS)] = (t_id == s_id).astype(F32)

    row_q, col_q = iota((ROWS, FR), 0), iota((ROWS, FR), 1)
    pick = (((row_q % FR) // 8) * 8 + row_q // FR == col_q).astype(BF)
    con = con_v[...].astype(F32).astype(BF)
    taken = dot(pick, con).astype(BF)
    inv_partners[...] = 1.0 / jnp.maximum(dot(taken, jnp.ones((CH, 128), BF)), 1.0)
    spread = (iota((CH, ROWS), 1) // FR == iota((CH, ROWS), 0)).astype(BF)
    same = iota((ROWS, ROWS), 0) % FR == iota((ROWS, ROWS), 1) % FR
    @pl.loop(0, CH)
    def _(k):
        @pl.when(k >= span)
        def _():
            s_in[k] = jnp.zeros((128, 128), BF)
            d_in[k] = jnp.ones((1, 128), F32)

    mix[...] = jnp.where(same, dot(taken, spread), 0.0).astype(BF)

    bias_row, gain_row = bias_v[...], gain_v[...]
    pending = []

    def send(one):
        one.start()
        pending.append(one)

    def wave_rows(d):
        return pl.ds(d * WAVE, WAVE)

    def part(d, slot, i, to):
        ref = feat.at[slot, wave_rows(d)]
        return pltpu.make_async_remote_copy(
            src_ref=ref, dst_ref=ref, send_sem=f_send.at[d, i], recv_sem=f_recv.at[d, i],
            device_id=(T, to), device_id_type=MESH,
        )

    def own_features(d):
        wait_bytes(rx.at[d], a_recv.at[d])
        feat[M, wave_rows(d)] = rx[d].reshape(256, WAVE).T
        send(part(d, M, 1, right))
        send(part(d, M, 2, left))
        send(part(d, M, 0, sib))

    def pass_on(d):
        for slot, i, to in ((left, 1, right), (right, 2, left)) if d % 2 == 0 else ((right, 2, left), (left, 1, right)):
            part(d, slot, i, sib).wait_recv()
            if (i == 1) == (d % 2 == 0):
                send(part(d, slot, 3, to))
            send(part(d, slot, 3 + i, sib))

    def pass_opposite(d):
        part(d, opp, 3, sib).wait_recv()
        send(part(d, opp, 6, sib))

    wait_bytes(w_v, w_sem)

    def add_projections(d, slots, first):
        rows = wave_rows(d)
        total = None if first else proj[rows, :]
        for slot in slots:
            term = dot(feat[slot, rows], w_v[slot].reshape(256, 640))
            total = term if total is None else total + term
        proj[rows, :] = total

    def project(d):
        part(d, sib, 0, sib).wait_recv()
        add_projections(d, (M, left, right, opp, sib), True)
        others = [2 * yy + 1 - core for yy in (left_y, right_y, opp_y)]
        for slot, i in zip(others, (4, 5, 6)):
            part(d, slot, i, sib).wait_recv()
        add_projections(d, others, False)

    def states(d):
        for s in (2 * d, 2 * d + 1):
            rows = pl.ds(s * FR, FR)
            logit = proj[rows, 384:512] + bias_row
            u = jnp.exp(-jnp.abs(logit))
            log1p = jnp.where(u < 1e-3, u * (1.0 - 0.5 * u), jnp.log(1.0 + u))
            log_decay = jnp.minimum(logit, 0.0) - log1p
            both = dot(tri, jnp.concatenate(split(log_decay), 1))
            total = both[:, :128] + both[:, 128:]
            decay_log[rows, :] = total
            seen = rcol[s]
            last, last_seen = total[FR - 1 :], seen[FR - 1 :]
            weight = jnp.where(seen == last_seen, jnp.exp(jnp.minimum(last - total, 0.0)), 0.0)
            state = dot3(proj[rows, 128:256] * weight, proj[rows, 256:384], ((0,), (0,)))
            decay = jnp.where(last_seen == 0.0, jnp.exp(last), 0.0)
            if s == 0:
                before[0] = jnp.ones((1, 128), F32)
                local_state[0] = jnp.zeros((128, 128), F32)
                after, product = state, decay
            else:
                after = local_state[s] * column(decay) + state
                product = before[s] * decay
            if s < CH - 1:
                local_state[s + 1] = after
                before[s + 1] = product
            else:
                s_own[...] = after.astype(BF)
                d_own[...] = product

    def gates(d):
        gate = proj[wave_rows(d), 512:640]
        gate_own[wave_rows(d)] = gate / (1.0 + jnp.exp(-gate))
        for s in (2 * d, 2 * d + 1):
            @pl.when(s != place)
            def _():
                piece(gate_own.at[pl.ds(s * FR, FR)], gate_in.at[char], gate_sem, span * CH + s).start()

    own_features(0)
    own_features(1)
    pass_on(0)
    pass_opposite(0)
    project(0)
    states(0)
    gates(0)
    own_features(2)
    pass_on(1)
    pass_opposite(1)
    project(1)
    states(1)
    gates(1)
    own_features(3)
    pass_on(2)
    pass_opposite(2)
    pass_on(3)
    project(2)
    states(2)
    gates(2)
    pass_opposite(3)
    project(3)
    states(3)

    def to_span(k):
        peer = holder(lax.rem(span + k, CH), char)
        return [
            pltpu.make_async_remote_copy(
                src_ref=src, dst_ref=dst.at[span], send_sem=sent.at[k], recv_sem=recv.at[span],
                device_id=(peer, M), device_id_type=MESH,
            )
            for src, dst, sent, recv in ((s_own, s_in, s_send, s_recv), (d_own, d_in, d_send, d_recv))
        ]

    for k in range(1, CH):
        @pl.when(span + k < CH)
        def _():
            for one in to_span(k):
                one.start()

    def to_owners(src, dst, sems):
        @pl.loop(1, CH)
        def _(k):
            to = lax.rem(place + k, CH)
            rows = pl.ds(pl.multiple_of(to * FR, FR), FR)
            piece(src.at[rows], dst.at[char], sems, span * CH + to).start()

        dst[char] = src[pl.ds(pl.multiple_of(place * FR, FR), FR)]

    gates(3)
    gate_in[char] = gate_own[pl.ds(pl.multiple_of(place * FR, FR), FR)]

    @pl.loop(0, CH)
    def _(c):
        rows = pl.ds(pl.multiple_of(c * FR, FR), FR)
        total = decay_log[rows, :]
        queries = proj[rows, 0:128] * HK ** (-0.5)
        keys, values = proj[rows, 128:256], proj[rows, 256:384]
        seen = rcol[c]
        carried = jnp.where(seen == 0.0, queries * jnp.exp(total), 0.0)
        carried_q[rows, :] = carried * before[c]
        picked = dot(sel[...], jnp.concatenate(split(total), 1))
        picked = picked[:, :128] + picked[:, 128:]
        scores = masks[len(LEVELS)] * dot3(queries, keys, ((1,), (1,)))
        for i in range(len(LEVELS)):
            gap = jnp.exp(-jnp.abs(total - picked[i * FR : (i + 1) * FR]))
            scores += masks[i] * dot3(queries * gap, keys * gap, ((1,), (1,)))
        scores = jnp.where(seen[:, :FR] == rrow[c], scores, 0.0)
        attended[rows, :] = dot3(scores, values) + dot3(carried, local_state[c])

    for k in range(CH - 1):
        @pl.when(k < span)
        def _():
            pltpu.make_async_copy(s_in.at[k], s_in.at[k], s_recv.at[k]).wait()
            pltpu.make_async_copy(d_in.at[k], d_in.at[k], d_recv.at[k]).wait()

    decays = d_in[...].reshape(CH, 128).T
    state = s_in[0].astype(F32)
    for k in range(1, CH - 1):
        state = state * decays[:, k : k + 1] + s_in[k].astype(F32)
    full = attended[...] + dot3(carried_q[...], state)
    square = jnp.mean(full * full, axis=-1, keepdims=True)
    norm_own[...] = (full * lax.rsqrt(square + 1e-06) * gain_row).astype(BF)
    to_owners(norm_own, norm_in, norm_sem)
    wait_bytes(gate_in.at[pl.ds(0, CH - 1)], gate_sem.at[1])
    silu = gate_in[...].reshape(ROWS, 128)
    wait_bytes(norm_in.at[pl.ds(0, CH - 1)], norm_sem.at[1])
    normed = norm_in[...].reshape(ROWS, 128).astype(F32)
    mixed = dot(mix[...], norm_in[...].reshape(ROWS, 128))
    gat[M] = ((normed + mixed * inv_partners[...]) * silu).astype(BF)

    half = ROWS // 2

    def gated_part(slot, h, i, to):
        ref = gat.at[slot, pl.ds(h * half, half)]
        return pltpu.make_async_remote_copy(
            src_ref=ref, dst_ref=ref, send_sem=g_send.at[i], recv_sem=g_recv.at[i],
            device_id=(T, to), device_id_type=MESH,
        )

    def go(*args):
        send(gated_part(*args))

    def arrived(slot, h, i):
        gated_part(slot, h, i, sib).wait_recv()

    def produce(m, first=False):
        rows = gat[m]
        term = dot(rows, ow_v[m])
        oacc[...] = term if first else oacc[...] + term
        part = dot(rows, cot_v[...], ((0,), (0,))).reshape(8, 16, 256)
        gradf[m] = part
        gbuf[m] = part.astype(BF)

    def along_x(to):
        @pl.when(to != x)
        def _():
            piece(gbuf.at[pl.ds(2 * to, 2)], xr.at[x], x_sem, to * NZ + z).start()

    go(M, 0, 2, right)
    go(M, 1, 5, left)
    go(M, 0, 0, sib)
    go(M, 1, 1, sib)
    go(M, 1, 3, right)
    go(M, 0, 4, left)
    produce(M, True)
    arrived(left, 0, 2)
    go(left, 0, 6, right)
    go(left, 0, 8, sib)
    arrived(right, 1, 5)
    go(right, 1, 7, left)
    go(right, 1, 11, sib)
    arrived(sib, 0, 0)
    arrived(sib, 1, 1)
    produce(sib)
    along_x(y)
    arrived(left, 1, 3)
    go(left, 1, 9, sib)
    arrived(right, 0, 4)
    go(right, 0, 10, sib)
    produce(left)
    arrived(opp, 0, 6)
    go(opp, 0, 12, sib)
    arrived(opp, 1, 7)
    go(opp, 1, 13, sib)
    produce(right)
    for yy, i in ((left_y, 8), (right_y, 10), (opp_y, 12)):
        slot = 2 * yy + 1 - core
        arrived(slot, 0, i)
        arrived(slot, 1, i + 1)
        if i == 12:
            produce(opp)
        produce(slot)
        along_x(yy)

    out_v[...] = oacc[...].astype(BF)
    store = pltpu.make_async_copy(out_v, out, out_sem.at[0])
    store.start()

    wait_bytes(xr.at[pl.ds(0, NX - 1)], x_sem.at[1])
    total = gradf[pl.ds(2 * x, 2)]
    for d in range(1, NX):
        total += xr[lax.rem(x + d, NX)].astype(F32)
    total = total.reshape(NZ, 16, 256)
    zf[...] = total
    zbuf[...] = total.astype(BF)

    @pl.loop(1, NZ)
    def _(k):
        to = lax.rem(z + k, NZ)
        piece(zbuf.at[to], zr.at[z], z_sem, x * NZ + to).start()

    wait_bytes(zr.at[pl.ds(0, NZ - 1)], z_sem.at[1])
    total = zf[z]
    for k in range(1, NZ):
        total += zr[lax.rem(z + k, NZ)].astype(F32)
    grad_v[...] = total
    last_store = pltpu.make_async_copy(grad_v, grad, out_sem.at[1])
    last_store.start()

    for d in range(NX):
        @pl.when(place == 0)
        def _():
            wait_bytes(rx.at[d, pl.ds(0, CH - 1)], a_send)

        @pl.when(place != 0)
        def _():
            wait_bytes(rx.at[d], a_send)

    wait_bytes(res_in.at[pl.ds(0, CH - 1)], r_sem.at[0])
    for one in pending:
        one.wait_send()
    for k in range(1, CH):
        @pl.when(span + k < CH)
        def _():
            for one in to_span(k):
                one.wait_send()

    wait_bytes(gate_in.at[pl.ds(0, CH - 1)], gate_sem.at[0])
    wait_bytes(norm_in.at[pl.ds(0, CH - 1)], norm_sem.at[0])
    wait_bytes(xr.at[pl.ds(0, NX - 1)], x_sem.at[0])
    wait_bytes(zbuf.at[pl.ds(0, NZ - 1)], z_sem.at[0])
    store.wait()
    last_store.wait()


def local(
    observations, contact, resets, q_weight, k_weight, v_weight, decay_weight, gate_weight,
    decay_bias, norm_gain, out_weight, out_cotangent,
):
    features = jnp.swapaxes(observations[0], 0, 1)
    weights = [
        w.reshape(8, MP, 32, 128) for w in (q_weight, k_weight, v_weight, decay_weight, gate_weight)
    ]
    vm = pltpu.VMEM
    dma = pltpu.SemaphoreType.DMA
    scratch = [
        vm((FR, CH), jnp.int32), vm((CH, FR), jnp.int32), vm((MP, 8, 32, 640), BF), vm((1, 128), F32),
        vm((1, 128), F32), vm((MP, 128, 256), BF), vm((ROWS, 256), BF),
        vm((NX, CH, 32, WAVE), BF), vm((MP, ROWS, 256), BF), vm((ROWS, 640), F32), vm((ROWS, 128), F32),
        vm((CH, 1, 128), F32), vm((CH, 1, 128), F32), vm((CH, FR, 128), F32), vm((CH, 1, FR), F32),
        vm((len(LEVELS) + 1, FR, FR), F32), vm((len(LEVELS) * FR, FR), BF),
        vm((ROWS, ROWS), BF), vm((ROWS, 128), F32),
        vm((CH, 128, 128), F32), vm((CH, 1, 128), F32), vm((128, 128), BF), vm((1, 128), F32),
        vm((CH, 128, 128), BF), vm((CH, 1, 128), F32), vm((ROWS, 128), F32), vm((ROWS, 128), F32),
        vm((ROWS, 128), F32), vm((CH, FR, 128), F32), vm((ROWS, 128), BF), vm((CH, FR, 128), BF),
        vm((MP, ROWS, 128), BF), vm((ROWS, 256), F32), vm((MP, 8, 16, 256), F32),
        vm((MP, 8, 16, 256), BF), vm((NX, 2, 8, 16, 256), BF), vm((NZ, 16, 256), F32),
        vm((NZ, 16, 256), BF), vm((NZ, 16, 256), BF), vm((ROWS, 256), BF), vm((16, 256), F32),
        dma((6,)), dma, dma((2,)), dma, dma((NX,)), dma((NX, 7)), dma((NX, 7)), dma((2,)),
        dma((CH,)), dma((CH,)), dma((CH,)), dma((CH,)), dma((2,)), dma((2,)), dma((14,)), dma((14,)), dma((2,)), dma((2,)),
    ]
    following, weight_grad = pl.pallas_call(
        kernel,
        out_shape=(
            jax.ShapeDtypeStruct((ROWS, 256), BF),
            jax.ShapeDtypeStruct((16, 256), F32),
        ),
        in_specs=[pl.BlockSpec(memory_space=pltpu.HBM)] * 12,
        out_specs=(pl.BlockSpec(memory_space=pltpu.HBM),) * 2,
        scratch_shapes=scratch,
        compiler_params=pltpu.CompilerParams(
            collective_id=0, has_side_effects=True, vmem_limit_bytes=60 * 2**20
        ),
    )(
        features, contact.reshape(FR, CH), resets, *weights, decay_bias, norm_gain,
        out_weight.reshape(MP, 128, 256), out_cotangent.reshape(ROWS, 256),
    )
    return following.reshape(CH, FR, 256), weight_grad


def solution(mesh):
    placed = (
        P("tm", None, "mp"),
        P("tm", None, None),
        P(None, "tm"),
        P(None, "mp"),
        P(None, "mp"),
        P(None, "mp"),
        P(None, "mp"),
        P(None, "mp"),
        P("mp", None),
        P("mp", None),
        P(None, "mp"),
        P(None, "tm", "mp"),
    )
    return jax.shard_map(
        local,
        mesh=mesh,
        in_specs=placed,
        out_specs=(P(None, "tm", "mp"), P("tm", "mp")),
        check_vma=False,
    )
```

```python
import jax
import jax.numpy as jnp
from jax import lax
from jax.experimental import pallas as pl
from jax.experimental.pallas import tpu as pltpu
from jax.sharding import PartitionSpec as P

MESH = pl.DeviceIdType.MESH
BF = jnp.bfloat16
F32 = jnp.float32

HK = 128
CH = 8
TM, MP = 64, 8
NX, NZ, NY = 4, 16, 4
FR = 64
ROWS = CH * FR
LEVELS = (32, 16, 8, 4, 2, 1)
WAVE = 2 * FR


def dot(a, b, dims=((1,), (0,))):
    return lax.dot_general(a, b, (dims, ((), ())), preferred_element_type=F32)


def split(a):
    high = a.astype(BF)
    return high, (a - high.astype(F32)).astype(BF)


def dot3(a, b, dims=((1,), (0,))):
    ah, al = split(a)
    bh, bl = split(b)
    da, db = dims[0][0], dims[1][0]
    return dot(jnp.concatenate([ah, al, ah], da), jnp.concatenate([bh, bh, bl], db), dims)


def iota(shape, dim):
    return lax.broadcasted_iota(jnp.int32, shape, dim)


def column(row):
    return jnp.broadcast_to(row, (8, 128)).T[:, :1]


def kernel(
    obs, contact, resets, wq, wk, wv, wd, wg, bias, gain, ow, cot,
    out, grad,
    con_v, res_v, w_v, bias_v, gain_v, ow_v, cot_v,
    rx, feat, proj, decay_log, res_own, res_in, rcol, rrow, masks, sel, mix, inv_partners,
    local_state, before, s_last, s_own, d_own, s_pair, d_pair, s_row, d_row, s_in, d_in, attended, carried_q,
    gate_own, gate_in, norm_own, norm_in,
    gat, oacc, gradf, gbuf, xr, zf, zbuf, zr, out_v, grad_v,
    in_sem, w_sem, out_sem, a_send, a_recv, f_send, f_recv, r_sem, e_send, e_recv, s_send, s_recv, d_send, d_recv,
    gate_sem, norm_sem, g_send, g_recv, x_sem, z_sem,
):
    T = lax.axis_index("tm")
    M = lax.axis_index("mp")
    x, z = T // NZ, lax.rem(T, NZ)
    y, core = M // 2, lax.rem(M, 2)
    span, place = T // CH, lax.rem(T, CH)
    half_row = lax.rem(span, 2)
    at_home = lax.rem(span + 2 * x, CH) == place

    def held(at):
        return lax.rem(at + CH - 2 * x, CH)

    char = held(place)

    def holder(other_span, other_char):
        return other_span * CH + lax.rem(other_char + 2 * (other_span // 2), CH)

    right_y, left_y, opp_y = lax.rem(y + 1, NY), lax.rem(y + 3, NY), lax.rem(y + 2, NY)

    def load(src, dst, i):
        return pltpu.make_async_copy(src, dst, in_sem.at[i])

    loads = [
        load(resets, res_v, 0), load(contact, con_v, 1), load(bias, bias_v, 2),
        load(gain, gain_v, 3), load(ow, ow_v, 4), load(cot, cot_v, 5),
    ]
    loads[0].start()

    barrier = pltpu.get_barrier_semaphore()

    @pl.loop(1, TM)
    def _(k):
        pl.semaphore_signal(barrier, inc=1, device_id=(lax.rem(T + k, TM), M), device_id_type=MESH)

    sib = 2 * y + 1 - core
    right, left, opp = 2 * right_y + core, 2 * left_y + core, 2 * opp_y + core
    for other in (sib, right, left):
        pl.semaphore_signal(barrier, inc=1, device_id=(T, other), device_id_type=MESH)

    for one in loads[1:]:
        one.start()

    @pl.loop(0, MP)
    def _(m):
        for j, w in enumerate((wq, wk, wv, wd, wg)):
            pltpu.make_async_copy(w.at[:, m], w_v.at[m, :, :, pl.ds(j * 128, 128)], w_sem).start()

    loads[0].wait()
    res = res_v[...].astype(F32)
    res = jnp.concatenate([res, jnp.zeros_like(res)], 1)
    for c in range(CH):
        res_own[c] = res[c : c + 1]
    res_in[place] = res_own[char]

    pl.semaphore_wait(barrier, TM - 1 + 3)

    def piece(src, dst, sems, peer):
        return pltpu.make_async_remote_copy(
            src_ref=src, dst_ref=dst, send_sem=sems.at[0], recv_sem=sems.at[1],
            device_id=(peer, M), device_id_type=MESH,
        )

    def wait_bytes(ref, sem):
        pltpu.make_async_copy(ref, ref, sem).wait()

    def piece_of_wave(src, dst, send, recv, d, peer):
        return pltpu.make_async_remote_copy(
            src_ref=src, dst_ref=dst, send_sem=send, recv_sem=recv.at[d],
            device_id=(peer, M), device_id_type=MESH,
        )

    def quarter(to, d):
        return obs.at[:, pl.ds(pl.multiple_of(to * CH * FR + d * WAVE, WAVE), WAVE)]

    for d in range(NX):
        @pl.loop(0, CH)
        def _(k):
            to = lax.rem(span + k, CH)
            peer = holder(to, span)

            @pl.when(peer != T)
            def _():
                pltpu.make_async_remote_copy(
                    src_ref=quarter(to, d), dst_ref=rx.at[d, place], send_sem=a_send, recv_sem=a_recv.at[d],
                    device_id=(peer, M), device_id_type=MESH,
                ).start()

        @pl.when(at_home)
        def _():
            pltpu.make_async_copy(quarter(span, d), rx.at[d, place], a_recv.at[d]).start()

    @pl.loop(1, CH)
    def _(k):
        to = lax.rem(place + k, CH)
        piece(res_own.at[held(to)], res_in.at[place], r_sem, span * CH + to).start()

    for one in loads[1:]:
        one.wait()
    tri = (iota((FR, FR), 0) >= iota((FR, FR), 1)).astype(BF)
    wait_bytes(res_in.at[pl.ds(0, CH - 1)], r_sem.at[1])
    res = res_in[...].reshape(CH, 128)[:, :FR].astype(BF)
    seen_col = dot(tri, res, ((1,), (1,)))
    seen_row = dot(res, tri, ((1,), (1,)))
    for c in range(CH):
        rcol[c] = jnp.broadcast_to(seen_col[:, c : c + 1], (FR, 128))
        rrow[c] = seen_row[c : c + 1, :]
    t_id, s_id = iota((FR, FR), 0), iota((FR, FR), 1)
    for i, h in enumerate(LEVELS):
        masks[i] = ((t_id // (2 * h) == s_id // (2 * h)) & (t_id // h > s_id // h)).astype(F32)
        sel[i * FR : (i + 1) * FR] = (s_id == (t_id // (2 * h)) * (2 * h) + h - 1).astype(BF)
    masks[len(LEVELS)] = (t_id == s_id).astype(F32)

    row_q, col_q = iota((ROWS, FR), 0), iota((ROWS, FR), 1)
    pick = (((row_q % FR) // 8) * 8 + row_q // FR == col_q).astype(BF)
    con = con_v[...].astype(F32).astype(BF)
    taken = dot(pick, con).astype(BF)
    inv_partners[...] = 1.0 / jnp.maximum(dot(taken, jnp.ones((CH, 128), BF)), 1.0)
    spread = (iota((CH, ROWS), 1) // FR == iota((CH, ROWS), 0)).astype(BF)
    same = iota((ROWS, ROWS), 0) % FR == iota((ROWS, ROWS), 1) % FR
    @pl.loop(0, NX)
    def _(k):
        @pl.when(k >= x)
        def _():
            s_in[k] = jnp.zeros((128, 128), BF)
            d_in[k] = jnp.ones((1, 128), F32)

    mix[...] = jnp.where(same, dot(taken, spread), 0.0).astype(BF)

    bias_row, gain_row = bias_v[...], gain_v[...]
    pending = []

    def send(one):
        one.start()
        pending.append(one)

    def wave_rows(d):
        return pl.ds(d * WAVE, WAVE)

    def part(d, slot, i, to):
        ref = feat.at[slot, wave_rows(d)]
        return pltpu.make_async_remote_copy(
            src_ref=ref, dst_ref=ref, send_sem=f_send.at[d, i], recv_sem=f_recv.at[d, i],
            device_id=(T, to), device_id_type=MESH,
        )

    def own_features(d):
        wait_bytes(rx.at[d], a_recv.at[d])
        feat[M, wave_rows(d)] = rx[d].reshape(256, WAVE).T
        send(part(d, M, 1, right))
        send(part(d, M, 2, left))
        send(part(d, M, 0, sib))

    def pass_on(d):
        for slot, i, to in ((left, 1, right), (right, 2, left)) if d % 2 == 0 else ((right, 2, left), (left, 1, right)):
            part(d, slot, i, sib).wait_recv()
            if (i == 1) == (d % 2 == 0):
                send(part(d, slot, 3, to))
            send(part(d, slot, 3 + i, sib))

    def pass_opposite(d):
        part(d, opp, 3, sib).wait_recv()
        send(part(d, opp, 6, sib))

    wait_bytes(w_v, w_sem)

    def add_projections(d, slots, first):
        rows = wave_rows(d)
        total = None if first else proj[rows, :]
        for slot in slots:
            term = dot(feat[slot, rows], w_v[slot].reshape(256, 640))
            total = term if total is None else total + term
        proj[rows, :] = total

    def project(d):
        part(d, sib, 0, sib).wait_recv()
        add_projections(d, (M, left, right, opp, sib), True)
        others = [2 * yy + 1 - core for yy in (left_y, right_y, opp_y)]
        for slot, i in zip(others, (4, 5, 6)):
            part(d, slot, i, sib).wait_recv()
        add_projections(d, others, False)

    def states(d):
        for s in (2 * d, 2 * d + 1):
            rows = pl.ds(s * FR, FR)
            logit = proj[rows, 384:512] + bias_row
            u = jnp.exp(-jnp.abs(logit))
            log1p = jnp.where(u < 1e-3, u * (1.0 - 0.5 * u), jnp.log(1.0 + u))
            log_decay = jnp.minimum(logit, 0.0) - log1p
            both = dot(tri, jnp.concatenate(split(log_decay), 1))
            total = both[:, :128] + both[:, 128:]
            decay_log[rows, :] = total
            seen = rcol[s]
            last, last_seen = total[FR - 1 :], seen[FR - 1 :]
            weight = jnp.where(seen == last_seen, jnp.exp(jnp.minimum(last - total, 0.0)), 0.0)
            state = dot3(proj[rows, 128:256] * weight, proj[rows, 256:384], ((0,), (0,)))
            decay = jnp.where(last_seen == 0.0, jnp.exp(last), 0.0)
            if s == 0:
                before[0] = jnp.ones((1, 128), F32)
                local_state[0] = jnp.zeros((128, 128), F32)
                after, product = state, decay
            else:
                after = local_state[s] * column(decay) + state
                product = before[s] * decay
            if s < CH - 1:
                local_state[s + 1] = after
                before[s + 1] = product
            else:
                s_last[...] = after
                s_own[...] = after.astype(BF)
                d_own[...] = product

    own_features(0)
    own_features(1)
    own_features(2)
    pass_on(0)
    own_features(3)
    pass_on(1)
    pass_opposite(0)
    pass_on(2)
    pass_opposite(1)
    pass_on(3)
    pass_opposite(2)
    project(0)
    pass_opposite(3)
    for d in range(NX):
        if d > 0:
            project(d)
        states(d)

    def exchange(i, src, dst, peer):
        return pltpu.make_async_remote_copy(
            src_ref=src, dst_ref=dst, send_sem=e_send.at[i], recv_sem=e_recv.at[i],
            device_id=(peer, M), device_id_type=MESH,
        )

    other = holder(span + 1 - 2 * half_row, char)
    swap = [exchange(0, s_own, s_pair, other), exchange(1, d_own, d_pair, other)]
    for one in swap:
        one.start()

    def to_owners(src, dst, sems):
        @pl.loop(1, CH)
        def _(k):
            to = lax.rem(place + k, CH)
            rows = pl.ds(pl.multiple_of(to * FR, FR), FR)
            piece(src.at[rows], dst.at[char], sems, span * CH + to).start()

        dst[char] = src[pl.ds(pl.multiple_of(place * FR, FR), FR)]

    for one in swap:
        one.wait_recv()
    upper = half_row == 1
    mine, theirs = s_last[...], s_pair[...].astype(F32)
    my_decay, their_decay = d_own[...], d_pair[...]
    late_decay = column(jnp.where(upper, my_decay, their_decay))
    s_row[...] = (late_decay * jnp.where(upper, theirs, mine) + jnp.where(upper, mine, theirs)).astype(BF)
    d_row[...] = my_decay * their_decay

    def to_row(k):
        peer = holder(lax.rem(span + 2 * k, CH), char)
        return [
            pltpu.make_async_remote_copy(
                src_ref=src, dst_ref=dst.at[x], send_sem=sent.at[k], recv_sem=recv.at[x],
                device_id=(peer, M), device_id_type=MESH,
            )
            for src, dst, sent, recv in ((s_row, s_in, s_send, s_recv), (d_row, d_in, d_send, d_recv))
        ]

    for k in range(1, NX):
        @pl.when(x + k < NX)
        def _():
            for one in to_row(k):
                one.start()

    gate = proj[:, 512:640]
    gate_own[...] = (gate / (1.0 + jnp.exp(-gate))).astype(BF)
    to_owners(gate_own, gate_in, gate_sem)

    @pl.loop(0, CH)
    def _(c):
        rows = pl.ds(pl.multiple_of(c * FR, FR), FR)
        total = decay_log[rows, :]
        queries = proj[rows, 0:128] * HK ** (-0.5)
        keys, values = proj[rows, 128:256], proj[rows, 256:384]
        seen = rcol[c]
        carried = jnp.where(seen == 0.0, queries * jnp.exp(total), 0.0)
        carried_q[rows, :] = carried * before[c]
        picked = dot(sel[...], jnp.concatenate(split(total), 1))
        picked = picked[:, :128] + picked[:, 128:]
        scores = masks[len(LEVELS)] * dot3(queries, keys, ((1,), (1,)))
        for i in range(len(LEVELS)):
            gap = jnp.exp(-jnp.abs(total - picked[i * FR : (i + 1) * FR]))
            scores += masks[i] * dot3(queries * gap, keys * gap, ((1,), (1,)))
        scores = jnp.where(seen[:, :FR] == rrow[c], scores, 0.0)
        attended[rows, :] = dot3(scores, values) + dot3(carried, local_state[c])

    for k in range(NX - 1):
        @pl.when(k < x)
        def _():
            pltpu.make_async_copy(s_in.at[k], s_in.at[k], s_recv.at[k]).wait()
            pltpu.make_async_copy(d_in.at[k], d_in.at[k], d_recv.at[k]).wait()

    state = s_in[0].astype(F32)
    for k in range(1, NX - 1):
        state = state * column(d_in[k]) + s_in[k].astype(F32)
    state = jnp.where(upper, state * column(d_pair[...]) + s_pair[...].astype(F32), state)
    full = attended[...] + dot3(carried_q[...], state)
    square = jnp.mean(full * full, axis=-1, keepdims=True)
    norm_own[...] = (full * lax.rsqrt(square + 1e-06) * gain_row).astype(BF)
    to_owners(norm_own, norm_in, norm_sem)
    wait_bytes(gate_in.at[pl.ds(0, CH - 1)], gate_sem.at[1])
    silu = gate_in[...].reshape(ROWS, 128).astype(F32)
    wait_bytes(norm_in.at[pl.ds(0, CH - 1)], norm_sem.at[1])
    normed = norm_in[...].reshape(ROWS, 128).astype(F32)
    mixed = dot(mix[...], norm_in[...].reshape(ROWS, 128))
    gat[M] = ((normed + mixed * inv_partners[...]) * silu).astype(BF)

    half = ROWS // 2

    def gated_part(slot, h, i, to):
        ref = gat.at[slot, pl.ds(h * half, half)]
        return pltpu.make_async_remote_copy(
            src_ref=ref, dst_ref=ref, send_sem=g_send.at[i], recv_sem=g_recv.at[i],
            device_id=(T, to), device_id_type=MESH,
        )

    def go(*args):
        send(gated_part(*args))

    def arrived(slot, h, i):
        gated_part(slot, h, i, sib).wait_recv()

    def produce(m, first=False):
        rows = gat[m]
        term = dot(rows, ow_v[m])
        oacc[...] = term if first else oacc[...] + term
        part = dot(rows, cot_v[...], ((0,), (0,))).reshape(8, 16, 256)
        gradf[m] = part
        gbuf[m] = part.astype(BF)

    def along_x(to):
        @pl.when(to != x)
        def _():
            piece(gbuf.at[pl.ds(2 * to, 2)], xr.at[x], x_sem, to * NZ + z).start()

    go(M, 0, 2, right)
    go(M, 1, 5, left)
    go(M, 0, 0, sib)
    go(M, 1, 1, sib)
    go(M, 1, 3, right)
    go(M, 0, 4, left)
    produce(M, True)
    arrived(left, 0, 2)
    go(left, 0, 6, right)
    go(left, 0, 8, sib)
    arrived(right, 1, 5)
    go(right, 1, 7, left)
    go(right, 1, 11, sib)
    arrived(sib, 0, 0)
    arrived(sib, 1, 1)
    produce(sib)
    along_x(y)
    arrived(left, 1, 3)
    go(left, 1, 9, sib)
    arrived(right, 0, 4)
    go(right, 0, 10, sib)
    produce(left)
    arrived(opp, 0, 6)
    go(opp, 0, 12, sib)
    arrived(opp, 1, 7)
    go(opp, 1, 13, sib)
    produce(right)
    for yy, i in ((left_y, 8), (right_y, 10), (opp_y, 12)):
        slot = 2 * yy + 1 - core
        arrived(slot, 0, i)
        arrived(slot, 1, i + 1)
        if i == 12:
            produce(opp)
        produce(slot)
        along_x(yy)

    out_v[...] = oacc[...].astype(BF)
    store = pltpu.make_async_copy(out_v, out, out_sem.at[0])
    store.start()

    wait_bytes(xr.at[pl.ds(0, NX - 1)], x_sem.at[1])
    total = gradf[pl.ds(2 * x, 2)]
    for d in range(1, NX):
        total += xr[lax.rem(x + d, NX)].astype(F32)
    total = total.reshape(NZ, 16, 256)
    zf[...] = total
    zbuf[...] = total.astype(BF)

    @pl.loop(1, NZ)
    def _(k):
        to = lax.rem(z + k, NZ)
        piece(zbuf.at[to], zr.at[z], z_sem, x * NZ + to).start()

    wait_bytes(zr.at[pl.ds(0, NZ - 1)], z_sem.at[1])
    total = zf[z]
    for k in range(1, NZ):
        total += zr[lax.rem(z + k, NZ)].astype(F32)
    grad_v[...] = total
    last_store = pltpu.make_async_copy(grad_v, grad, out_sem.at[1])
    last_store.start()

    for d in range(NX):
        @pl.when(at_home)
        def _():
            wait_bytes(rx.at[d, pl.ds(0, CH - 1)], a_send)

        @pl.when(jnp.logical_not(at_home))
        def _():
            wait_bytes(rx.at[d], a_send)

    wait_bytes(res_in.at[pl.ds(0, CH - 1)], r_sem.at[0])
    for one in pending:
        one.wait_send()
    for one in swap:
        one.wait_send()
    for k in range(1, NX):
        @pl.when(x + k < NX)
        def _():
            for one in to_row(k):
                one.wait_send()

    wait_bytes(gate_in.at[pl.ds(0, CH - 1)], gate_sem.at[0])
    wait_bytes(norm_in.at[pl.ds(0, CH - 1)], norm_sem.at[0])
    wait_bytes(xr.at[pl.ds(0, NX - 1)], x_sem.at[0])
    wait_bytes(zbuf.at[pl.ds(0, NZ - 1)], z_sem.at[0])
    store.wait()
    last_store.wait()


def local(
    observations, contact, resets, q_weight, k_weight, v_weight, decay_weight, gate_weight,
    decay_bias, norm_gain, out_weight, out_cotangent,
):
    features = jnp.swapaxes(observations[0], 0, 1)
    weights = [
        w.reshape(8, MP, 32, 128) for w in (q_weight, k_weight, v_weight, decay_weight, gate_weight)
    ]
    vm = pltpu.VMEM
    dma = pltpu.SemaphoreType.DMA
    scratch = [
        vm((FR, CH), jnp.int32), vm((CH, FR), jnp.int32), vm((MP, 8, 32, 640), BF), vm((1, 128), F32),
        vm((1, 128), F32), vm((MP, 128, 256), BF), vm((ROWS, 256), BF),
        vm((NX, CH, 32, WAVE), BF), vm((MP, ROWS, 256), BF), vm((ROWS, 640), F32), vm((ROWS, 128), F32),
        vm((CH, 1, 128), F32), vm((CH, 1, 128), F32), vm((CH, FR, 128), F32), vm((CH, 1, FR), F32),
        vm((len(LEVELS) + 1, FR, FR), F32), vm((len(LEVELS) * FR, FR), BF),
        vm((ROWS, ROWS), BF), vm((ROWS, 128), F32),
        vm((CH, 128, 128), F32), vm((CH, 1, 128), F32), vm((128, 128), F32),
        vm((128, 128), BF), vm((1, 128), F32), vm((128, 128), BF), vm((1, 128), F32),
        vm((128, 128), BF), vm((1, 128), F32), vm((NX, 128, 128), BF), vm((NX, 1, 128), F32), vm((ROWS, 128), F32), vm((ROWS, 128), F32),
        vm((ROWS, 128), BF), vm((CH, FR, 128), BF), vm((ROWS, 128), BF), vm((CH, FR, 128), BF),
        vm((MP, ROWS, 128), BF), vm((ROWS, 256), F32), vm((MP, 8, 16, 256), F32),
        vm((MP, 8, 16, 256), BF), vm((NX, 2, 8, 16, 256), BF), vm((NZ, 16, 256), F32),
        vm((NZ, 16, 256), BF), vm((NZ, 16, 256), BF), vm((ROWS, 256), BF), vm((16, 256), F32),
        dma((6,)), dma, dma((2,)), dma, dma((NX,)), dma((NX, 7)), dma((NX, 7)), dma((2,)),
        dma((2,)), dma((2,)), dma((NX,)), dma((NX,)), dma((NX,)), dma((NX,)), dma((2,)), dma((2,)), dma((14,)), dma((14,)), dma((2,)), dma((2,)),
    ]
    following, weight_grad = pl.pallas_call(
        kernel,
        out_shape=(
            jax.ShapeDtypeStruct((ROWS, 256), BF),
            jax.ShapeDtypeStruct((16, 256), F32),
        ),
        in_specs=[pl.BlockSpec(memory_space=pltpu.HBM)] * 12,
        out_specs=(pl.BlockSpec(memory_space=pltpu.HBM),) * 2,
        scratch_shapes=scratch,
        compiler_params=pltpu.CompilerParams(
            collective_id=0, has_side_effects=True, vmem_limit_bytes=60 * 2**20
        ),
    )(
        features, contact.reshape(FR, CH), resets, *weights, decay_bias, norm_gain,
        out_weight.reshape(MP, 128, 256), out_cotangent.reshape(ROWS, 256),
    )
    return following.reshape(CH, FR, 256), weight_grad


def solution(mesh):
    placed = (
        P("tm", None, "mp"),
        P("tm", None, None),
        P(None, "tm"),
        P(None, "mp"),
        P(None, "mp"),
        P(None, "mp"),
        P(None, "mp"),
        P(None, "mp"),
        P("mp", None),
        P("mp", None),
        P(None, "mp"),
        P(None, "tm", "mp"),
    )
    return jax.shard_map(
        local,
        mesh=mesh,
        in_specs=placed,
        out_specs=(P(None, "tm", "mp"), P("tm", "mp")),
        check_vma=False,
    )
```

```python
import jax
import jax.numpy as jnp
from jax import lax
from jax.experimental import pallas as pl
from jax.experimental.pallas import tpu as pltpu
from jax.sharding import PartitionSpec as P

MESH = pl.DeviceIdType.MESH
BF = jnp.bfloat16
F32 = jnp.float32

HK = 128
CH = 8
TM, MP = 64, 8
NX, NZ, NY = 4, 16, 4
FR = 64
ROWS = CH * FR
LEVELS = (32, 16, 8, 4, 2, 1)
WAVE = 2 * FR


def dot(a, b, dims=((1,), (0,))):
    return lax.dot_general(a, b, (dims, ((), ())), preferred_element_type=F32)


def split(a):
    high = a.astype(BF)
    return high, (a - high.astype(F32)).astype(BF)


def dot3(a, b, dims=((1,), (0,))):
    ah, al = split(a)
    bh, bl = split(b)
    da, db = dims[0][0], dims[1][0]
    return dot(jnp.concatenate([ah, al, ah], da), jnp.concatenate([bh, bh, bl], db), dims)


def iota(shape, dim):
    return lax.broadcasted_iota(jnp.int32, shape, dim)


def column(row):
    return jnp.broadcast_to(row, (8, 128)).T[:, :1]


def kernel(
    obs, contact, resets, wq, wk, wv, wd, wg, bias, gain, ow, cot,
    out, grad,
    con_v, res_v, w_v, bias_v, gain_v, ow_v, cot_v,
    rx, feat, proj, decay_log, res_own, res_in, rcol, rrow, masks, sel, mix, inv_partners,
    local_state, before, s_last, s_own, d_own, s_pair, d_pair, s_row, d_row, s_in, d_in, attended, carried_q,
    gate_own, gate_in, norm_own, norm_in,
    gat, oacc, gradf, gbuf, xr, zf, zbuf, zr, out_v, grad_v,
    in_sem, w_sem, out_sem, a_send, a_recv, f_send, f_recv, r_sem, e_send, e_recv, s_send, s_recv, d_send, d_recv,
    gate_sem, norm_sem, g_send, g_recv, x_send, x_recv, z_sem,
):
    T = lax.axis_index("tm")
    M = lax.axis_index("mp")
    x, z = T // NZ, lax.rem(T, NZ)
    y, core = M // 2, lax.rem(M, 2)
    span, place = T // CH, lax.rem(T, CH)
    half_row = lax.rem(span, 2)
    at_home = lax.rem(span + 2 * x, CH) == place

    def held(at):
        return lax.rem(at + CH - 2 * x, CH)

    char = held(place)

    def holder(other_span, other_char):
        return other_span * CH + lax.rem(other_char + 2 * (other_span // 2), CH)

    right_y, left_y, opp_y = lax.rem(y + 1, NY), lax.rem(y + 3, NY), lax.rem(y + 2, NY)

    def load(src, dst, i):
        return pltpu.make_async_copy(src, dst, in_sem.at[i])

    loads = [
        load(resets, res_v, 0), load(contact, con_v, 1), load(bias, bias_v, 2),
        load(gain, gain_v, 3), load(ow, ow_v, 4), load(cot, cot_v, 5),
    ]
    loads[0].start()

    barrier = pltpu.get_barrier_semaphore()

    @pl.loop(1, TM)
    def _(k):
        pl.semaphore_signal(barrier, inc=1, device_id=(lax.rem(T + k, TM), M), device_id_type=MESH)

    sib = 2 * y + 1 - core
    right, left, opp = 2 * right_y + core, 2 * left_y + core, 2 * opp_y + core
    for other in (sib, right, left):
        pl.semaphore_signal(barrier, inc=1, device_id=(T, other), device_id_type=MESH)

    for one in loads[1:]:
        one.start()

    @pl.loop(0, MP)
    def _(m):
        for j, w in enumerate((wq, wk, wv, wd, wg)):
            pltpu.make_async_copy(w.at[:, m], w_v.at[m, :, :, pl.ds(j * 128, 128)], w_sem).start()

    loads[0].wait()
    res = res_v[...].astype(F32)
    res = jnp.concatenate([res, jnp.zeros_like(res)], 1)
    for c in range(CH):
        res_own[c] = res[c : c + 1]
    res_in[place] = res_own[char]

    pl.semaphore_wait(barrier, TM - 1 + 3)

    def piece(src, dst, sems, peer):
        return pltpu.make_async_remote_copy(
            src_ref=src, dst_ref=dst, send_sem=sems.at[0], recv_sem=sems.at[1],
            device_id=(peer, M), device_id_type=MESH,
        )

    def wait_bytes(ref, sem):
        pltpu.make_async_copy(ref, ref, sem).wait()

    def piece_of_wave(src, dst, send, recv, d, peer):
        return pltpu.make_async_remote_copy(
            src_ref=src, dst_ref=dst, send_sem=send, recv_sem=recv.at[d],
            device_id=(peer, M), device_id_type=MESH,
        )

    def quarter(to, d):
        return obs.at[:, pl.ds(pl.multiple_of(to * CH * FR + d * WAVE, WAVE), WAVE)]

    for d in range(NX):
        @pl.loop(0, CH)
        def _(k):
            to = lax.rem(span + k, CH)
            peer = holder(to, span)

            @pl.when(peer != T)
            def _():
                pltpu.make_async_remote_copy(
                    src_ref=quarter(to, d), dst_ref=rx.at[d, place], send_sem=a_send, recv_sem=a_recv.at[d],
                    device_id=(peer, M), device_id_type=MESH,
                ).start()

        @pl.when(at_home)
        def _():
            pltpu.make_async_copy(quarter(span, d), rx.at[d, place], a_recv.at[d]).start()

    @pl.loop(1, CH)
    def _(k):
        to = lax.rem(place + k, CH)
        piece(res_own.at[held(to)], res_in.at[place], r_sem, span * CH + to).start()

    for one in loads[1:]:
        one.wait()
    tri = (iota((FR, FR), 0) >= iota((FR, FR), 1)).astype(BF)
    wait_bytes(res_in.at[pl.ds(0, CH - 1)], r_sem.at[1])
    res = res_in[...].reshape(CH, 128)[:, :FR].astype(BF)
    seen_col = dot(tri, res, ((1,), (1,)))
    seen_row = dot(res, tri, ((1,), (1,)))
    for c in range(CH):
        rcol[c] = jnp.broadcast_to(seen_col[:, c : c + 1], (FR, 128))
        rrow[c] = seen_row[c : c + 1, :]
    t_id, s_id = iota((FR, FR), 0), iota((FR, FR), 1)
    for i, h in enumerate(LEVELS):
        masks[i] = ((t_id // (2 * h) == s_id // (2 * h)) & (t_id // h > s_id // h)).astype(F32)
        sel[i * FR : (i + 1) * FR] = (s_id == (t_id // (2 * h)) * (2 * h) + h - 1).astype(BF)
    masks[len(LEVELS)] = (t_id == s_id).astype(F32)

    row_q, col_q = iota((ROWS, FR), 0), iota((ROWS, FR), 1)
    pick = (((row_q % FR) // 8) * 8 + row_q // FR == col_q).astype(BF)
    con = con_v[...].astype(F32).astype(BF)
    taken = dot(pick, con).astype(BF)
    inv_partners[...] = 1.0 / jnp.maximum(dot(taken, jnp.ones((CH, 128), BF)), 1.0)
    spread = (iota((CH, ROWS), 1) // FR == iota((CH, ROWS), 0)).astype(BF)
    same = iota((ROWS, ROWS), 0) % FR == iota((ROWS, ROWS), 1) % FR
    @pl.loop(0, NX)
    def _(k):
        @pl.when(k >= x)
        def _():
            s_in[k] = jnp.zeros((128, 128), BF)
            d_in[k] = jnp.ones((1, 128), F32)

    mix[...] = jnp.where(same, dot(taken, spread), 0.0).astype(BF)

    bias_row, gain_row = bias_v[...], gain_v[...]
    pending = []

    def send(one):
        one.start()
        pending.append(one)

    def wave_rows(d):
        return pl.ds(d * WAVE, WAVE)

    def part(d, slot, i, to):
        ref = feat.at[slot, wave_rows(d)]
        return pltpu.make_async_remote_copy(
            src_ref=ref, dst_ref=ref, send_sem=f_send.at[d, i], recv_sem=f_recv.at[d, i],
            device_id=(T, to), device_id_type=MESH,
        )

    def own_features(d):
        wait_bytes(rx.at[d], a_recv.at[d])
        feat[M, wave_rows(d)] = rx[d].reshape(256, WAVE).T
        send(part(d, M, 1, right))
        send(part(d, M, 2, left))
        send(part(d, M, 0, sib))

    def pass_on(d):
        for slot, i, to in ((left, 1, right), (right, 2, left)) if d % 2 == 0 else ((right, 2, left), (left, 1, right)):
            part(d, slot, i, sib).wait_recv()
            if (i == 1) == (d % 2 == 0):
                send(part(d, slot, 3, to))
            send(part(d, slot, 3 + i, sib))

    def pass_opposite(d):
        part(d, opp, 3, sib).wait_recv()
        send(part(d, opp, 6, sib))

    wait_bytes(w_v, w_sem)

    def add_projections(d, slots, first):
        rows = wave_rows(d)
        total = None if first else proj[rows, :]
        for slot in slots:
            term = dot(feat[slot, rows], w_v[slot].reshape(256, 640))
            total = term if total is None else total + term
        proj[rows, :] = total

    def project(d):
        part(d, sib, 0, sib).wait_recv()
        add_projections(d, (M, left, right, opp, sib), True)
        others = [2 * yy + 1 - core for yy in (left_y, right_y, opp_y)]
        for slot, i in zip(others, (4, 5, 6)):
            part(d, slot, i, sib).wait_recv()
        add_projections(d, others, False)

    def states(d):
        for s in (2 * d, 2 * d + 1):
            rows = pl.ds(s * FR, FR)
            logit = proj[rows, 384:512] + bias_row
            u = jnp.exp(-jnp.abs(logit))
            log1p = jnp.where(u < 1e-3, u * (1.0 - 0.5 * u), jnp.log(1.0 + u))
            log_decay = jnp.minimum(logit, 0.0) - log1p
            both = dot(tri, jnp.concatenate(split(log_decay), 1))
            total = both[:, :128] + both[:, 128:]
            decay_log[rows, :] = total
            seen = rcol[s]
            last, last_seen = total[FR - 1 :], seen[FR - 1 :]
            weight = jnp.where(seen == last_seen, jnp.exp(jnp.minimum(last - total, 0.0)), 0.0)
            state = dot3(proj[rows, 128:256] * weight, proj[rows, 256:384], ((0,), (0,)))
            decay = jnp.where(last_seen == 0.0, jnp.exp(last), 0.0)
            if s == 0:
                before[0] = jnp.ones((1, 128), F32)
                local_state[0] = jnp.zeros((128, 128), F32)
                after, product = state, decay
            else:
                after = local_state[s] * column(decay) + state
                product = before[s] * decay
            if s < CH - 1:
                local_state[s + 1] = after
                before[s + 1] = product
            else:
                s_last[...] = after
                s_own[...] = after.astype(BF)
                d_own[...] = product

    own_features(0)
    own_features(1)
    own_features(2)
    pass_on(0)
    own_features(3)
    pass_on(1)
    pass_opposite(0)
    pass_on(2)
    pass_opposite(1)
    pass_on(3)
    pass_opposite(2)
    project(0)
    pass_opposite(3)
    for d in range(NX):
        if d > 0:
            project(d)
        states(d)

    def inside(low, high):
        @pl.loop(low, high)
        def _(c):
            inside_one(c)

    def inside_one(c):
        rows = pl.ds(pl.multiple_of(c * FR, FR), FR)
        total = decay_log[rows, :]
        queries = proj[rows, 0:128] * HK ** (-0.5)
        keys, values = proj[rows, 128:256], proj[rows, 256:384]
        seen = rcol[c]
        carried = jnp.where(seen == 0.0, queries * jnp.exp(total), 0.0)
        carried_q[rows, :] = carried * before[c]
        picked = dot(sel[...], jnp.concatenate(split(total), 1))
        picked = picked[:, :128] + picked[:, 128:]
        scores = masks[len(LEVELS)] * dot3(queries, keys, ((1,), (1,)))
        for i in range(len(LEVELS)):
            gap = jnp.exp(-jnp.abs(total - picked[i * FR : (i + 1) * FR]))
            scores += masks[i] * dot3(queries * gap, keys * gap, ((1,), (1,)))
        scores = jnp.where(seen[:, :FR] == rrow[c], scores, 0.0)
        attended[rows, :] = dot3(scores, values) + dot3(carried, local_state[c])

    def exchange(i, src, dst, peer):
        return pltpu.make_async_remote_copy(
            src_ref=src, dst_ref=dst, send_sem=e_send.at[i], recv_sem=e_recv.at[i],
            device_id=(peer, M), device_id_type=MESH,
        )

    other = holder(span + 1 - 2 * half_row, char)
    swap = [exchange(0, s_own, s_pair, other), exchange(1, d_own, d_pair, other)]
    for one in swap:
        one.start()

    inside(0, 6)
    gate = proj[:, 512:640]
    gate_own[...] = (gate / (1.0 + jnp.exp(-gate))).astype(BF)

    def to_owners(src, dst, sems):
        @pl.loop(1, CH)
        def _(k):
            to = lax.rem(place + k, CH)
            rows = pl.ds(pl.multiple_of(to * FR, FR), FR)
            piece(src.at[rows], dst.at[char], sems, span * CH + to).start()

        dst[char] = src[pl.ds(pl.multiple_of(place * FR, FR), FR)]

    for one in swap:
        one.wait_recv()
    upper = half_row == 1
    mine, theirs = s_last[...], s_pair[...].astype(F32)
    my_decay, their_decay = d_own[...], d_pair[...]
    late_decay = column(jnp.where(upper, my_decay, their_decay))
    s_row[...] = (late_decay * jnp.where(upper, theirs, mine) + jnp.where(upper, mine, theirs)).astype(BF)
    d_row[...] = my_decay * their_decay

    def to_row(k):
        peer = holder(lax.rem(span + 2 * k, CH), char)
        return [
            pltpu.make_async_remote_copy(
                src_ref=src, dst_ref=dst.at[x], send_sem=sent.at[k], recv_sem=recv.at[x],
                device_id=(peer, M), device_id_type=MESH,
            )
            for src, dst, sent, recv in ((s_row, s_in, s_send, s_recv), (d_row, d_in, d_send, d_recv))
        ]

    for k in range(1, NX):
        @pl.when(x + k < NX)
        def _():
            for one in to_row(k):
                one.start()

    to_owners(gate_own, gate_in, gate_sem)

    inside(6, CH)

    for k in range(NX - 1):
        @pl.when(k < x)
        def _():
            pltpu.make_async_copy(s_in.at[k], s_in.at[k], s_recv.at[k]).wait()
            pltpu.make_async_copy(d_in.at[k], d_in.at[k], d_recv.at[k]).wait()

    state = s_in[0].astype(F32)
    for k in range(1, NX - 1):
        state = state * column(d_in[k]) + s_in[k].astype(F32)
    state = jnp.where(upper, state * column(d_pair[...]) + s_pair[...].astype(F32), state)
    full = attended[...] + dot3(carried_q[...], state)
    square = jnp.mean(full * full, axis=-1, keepdims=True)
    norm_own[...] = (full * lax.rsqrt(square + 1e-06) * gain_row).astype(BF)
    to_owners(norm_own, norm_in, norm_sem)
    wait_bytes(gate_in.at[pl.ds(0, CH - 1)], gate_sem.at[1])
    silu = gate_in[...].reshape(ROWS, 128).astype(F32)
    wait_bytes(norm_in.at[pl.ds(0, CH - 1)], norm_sem.at[1])
    normed = norm_in[...].reshape(ROWS, 128).astype(F32)
    mixed = dot(mix[...], norm_in[...].reshape(ROWS, 128))
    gat[M] = ((normed + mixed * inv_partners[...]) * silu).astype(BF)

    half = ROWS // 2

    def gated_part(slot, h, i, to):
        ref = gat.at[slot, pl.ds(h * half, half)]
        return pltpu.make_async_remote_copy(
            src_ref=ref, dst_ref=ref, send_sem=g_send.at[i], recv_sem=g_recv.at[i],
            device_id=(T, to), device_id_type=MESH,
        )

    def go(*args):
        send(gated_part(*args))

    def arrived(slot, h, i):
        gated_part(slot, h, i, sib).wait_recv()

    def along_x(m):
        to, j = m // 2, lax.rem(m, 2)
        return pltpu.make_async_remote_copy(
            src_ref=gbuf.at[m], dst_ref=xr.at[j, x], send_sem=x_send, recv_sem=x_recv.at[j],
            device_id=(to * NZ + z, M), device_id_type=MESH,
        )

    def produce(m, first=False):
        rows = gat[m]
        part = dot(rows, cot_v[...], ((0,), (0,))).reshape(8, 16, 256)
        gradf[m] = part
        gbuf[m] = part.astype(BF)

        @pl.when(m // 2 != x)
        def _():
            along_x(m).start()

        term = dot(rows, ow_v[m])
        oacc[...] = term if first else oacc[...] + term

    go(M, 0, 2, right)
    go(M, 1, 5, left)
    go(M, 0, 0, sib)
    go(M, 1, 1, sib)
    go(M, 1, 3, right)
    go(M, 0, 4, left)
    produce(M, True)
    arrived(left, 0, 2)
    go(left, 0, 6, right)
    go(left, 0, 8, sib)
    arrived(right, 1, 5)
    go(right, 1, 7, left)
    go(right, 1, 11, sib)
    arrived(sib, 0, 0)
    arrived(sib, 1, 1)
    arrived(left, 1, 3)
    go(left, 1, 9, sib)
    arrived(right, 0, 4)
    go(right, 0, 10, sib)
    produce(left)
    produce(right)
    arrived(opp, 0, 6)
    go(opp, 0, 12, sib)
    arrived(opp, 1, 7)
    go(opp, 1, 13, sib)
    produce(opp)
    produce(sib)
    for yy, i in ((left_y, 8), (right_y, 10), (opp_y, 12)):
        slot = 2 * yy + 1 - core
        arrived(slot, 0, i)
        arrived(slot, 1, i + 1)
        produce(slot)

    out_v[...] = oacc[...].astype(BF)
    store = pltpu.make_async_copy(out_v, out, out_sem.at[0])
    store.start()

    for j in (core, 1 - core):
        wait_bytes(xr.at[j, pl.ds(0, NX - 1)], x_recv.at[j])
        total = gradf[2 * x + j]
        for d in range(1, NX):
            total += xr[j, lax.rem(x + d, NX)].astype(F32)
        owners = pl.ds(j * 8, 8)
        zf[owners] = total
        zbuf[owners] = total.astype(BF)

        @pl.loop(0, 8)
        def _(k):
            to = j * 8 + lax.rem(z + k, 8)

            @pl.when(to != z)
            def _():
                piece(zbuf.at[to], zr.at[z], z_sem, x * NZ + to).start()

    wait_bytes(zr.at[pl.ds(0, NZ - 1)], z_sem.at[1])
    total = zf[z]
    for k in range(1, NZ):
        total += zr[lax.rem(z + k, NZ)].astype(F32)
    grad_v[...] = total
    last_store = pltpu.make_async_copy(grad_v, grad, out_sem.at[1])
    last_store.start()

    for d in range(NX):
        @pl.when(at_home)
        def _():
            wait_bytes(rx.at[d, pl.ds(0, CH - 1)], a_send)

        @pl.when(jnp.logical_not(at_home))
        def _():
            wait_bytes(rx.at[d], a_send)

    wait_bytes(res_in.at[pl.ds(0, CH - 1)], r_sem.at[0])
    for one in pending:
        one.wait_send()
    for one in swap:
        one.wait_send()
    for k in range(1, NX):
        @pl.when(x + k < NX)
        def _():
            for one in to_row(k):
                one.wait_send()

    wait_bytes(gate_in.at[pl.ds(0, CH - 1)], gate_sem.at[0])
    wait_bytes(norm_in.at[pl.ds(0, CH - 1)], norm_sem.at[0])
    for j in range(2):
        wait_bytes(xr.at[j, pl.ds(0, NX - 1)], x_send)
    wait_bytes(zbuf.at[pl.ds(0, NZ - 1)], z_sem.at[0])
    store.wait()
    last_store.wait()


def local(
    observations, contact, resets, q_weight, k_weight, v_weight, decay_weight, gate_weight,
    decay_bias, norm_gain, out_weight, out_cotangent,
):
    features = jnp.swapaxes(observations[0], 0, 1)
    weights = [
        w.reshape(8, MP, 32, 128) for w in (q_weight, k_weight, v_weight, decay_weight, gate_weight)
    ]
    vm = pltpu.VMEM
    dma = pltpu.SemaphoreType.DMA
    scratch = [
        vm((FR, CH), jnp.int32), vm((CH, FR), jnp.int32), vm((MP, 8, 32, 640), BF), vm((1, 128), F32),
        vm((1, 128), F32), vm((MP, 128, 256), BF), vm((ROWS, 256), BF),
        vm((NX, CH, 32, WAVE), BF), vm((MP, ROWS, 256), BF), vm((ROWS, 640), F32), vm((ROWS, 128), F32),
        vm((CH, 1, 128), F32), vm((CH, 1, 128), F32), vm((CH, FR, 128), F32), vm((CH, 1, FR), F32),
        vm((len(LEVELS) + 1, FR, FR), F32), vm((len(LEVELS) * FR, FR), BF),
        vm((ROWS, ROWS), BF), vm((ROWS, 128), F32),
        vm((CH, 128, 128), F32), vm((CH, 1, 128), F32), vm((128, 128), F32),
        vm((128, 128), BF), vm((1, 128), F32), vm((128, 128), BF), vm((1, 128), F32),
        vm((128, 128), BF), vm((1, 128), F32), vm((NX, 128, 128), BF), vm((NX, 1, 128), F32), vm((ROWS, 128), F32), vm((ROWS, 128), F32),
        vm((ROWS, 128), BF), vm((CH, FR, 128), BF), vm((ROWS, 128), BF), vm((CH, FR, 128), BF),
        vm((MP, ROWS, 128), BF), vm((ROWS, 256), F32), vm((MP, 8, 16, 256), F32),
        vm((MP, 8, 16, 256), BF), vm((2, NX, 8, 16, 256), BF), vm((NZ, 16, 256), F32),
        vm((NZ, 16, 256), BF), vm((NZ, 16, 256), BF), vm((ROWS, 256), BF), vm((16, 256), F32),
        dma((6,)), dma, dma((2,)), dma, dma((NX,)), dma((NX, 7)), dma((NX, 7)), dma((2,)),
        dma((2,)), dma((2,)), dma((NX,)), dma((NX,)), dma((NX,)), dma((NX,)), dma((2,)), dma((2,)), dma((14,)), dma((14,)), dma, dma((2,)), dma((2,)),
    ]
    following, weight_grad = pl.pallas_call(
        kernel,
        out_shape=(
            jax.ShapeDtypeStruct((ROWS, 256), BF),
            jax.ShapeDtypeStruct((16, 256), F32),
        ),
        in_specs=[pl.BlockSpec(memory_space=pltpu.HBM)] * 12,
        out_specs=(pl.BlockSpec(memory_space=pltpu.HBM),) * 2,
        scratch_shapes=scratch,
        compiler_params=pltpu.CompilerParams(
            collective_id=0, has_side_effects=True, vmem_limit_bytes=60 * 2**20
        ),
    )(
        features, contact.reshape(FR, CH), resets, *weights, decay_bias, norm_gain,
        out_weight.reshape(MP, 128, 256), out_cotangent.reshape(ROWS, 256),
    )
    return following.reshape(CH, FR, 256), weight_grad


def solution(mesh):
    placed = (
        P("tm", None, "mp"),
        P("tm", None, None),
        P(None, "tm"),
        P(None, "mp"),
        P(None, "mp"),
        P(None, "mp"),
        P(None, "mp"),
        P(None, "mp"),
        P("mp", None),
        P("mp", None),
        P(None, "mp"),
        P(None, "tm", "mp"),
    )
    return jax.shard_map(
        local,
        mesh=mesh,
        in_specs=placed,
        out_specs=(P(None, "tm", "mp"), P("tm", "mp")),
        check_vma=False,
    )
```

```python
import jax
import jax.numpy as jnp
from jax import lax
from jax.experimental import pallas as pl
from jax.experimental.pallas import tpu as pltpu
from jax.sharding import PartitionSpec as P

MESH = pl.DeviceIdType.MESH
BF = jnp.bfloat16
F32 = jnp.float32

HK = 128
CH = 8
TM, MP = 64, 8
NX, NZ, NY = 4, 16, 4
FR = 64
ROWS = CH * FR
LEVELS = (32, 16, 8, 4, 2, 1)
WAVE = 2 * FR


def dot(a, b, dims=((1,), (0,))):
    return lax.dot_general(a, b, (dims, ((), ())), preferred_element_type=F32)


def split(a):
    high = a.astype(BF)
    return high, (a - high.astype(F32)).astype(BF)


def dot3(a, b, dims=((1,), (0,))):
    ah, al = split(a)
    bh, bl = split(b)
    da, db = dims[0][0], dims[1][0]
    return dot(jnp.concatenate([ah, al, ah], da), jnp.concatenate([bh, bh, bl], db), dims)


def iota(shape, dim):
    return lax.broadcasted_iota(jnp.int32, shape, dim)


def column(row):
    return jnp.broadcast_to(row, (8, 128)).T[:, :1]


def kernel(
    obs, contact, resets, wq, wk, wv, wd, wg, bias, gain, ow, cot,
    out, grad,
    con_v, res_v, w_v, bias_v, gain_v, ow_v, cot_v,
    rx, feat, proj, decay_log, res_own, res_in, rcol, rrow, masks, sel, mix, inv_partners,
    local_state, before, s_last, s_own, d_own, s_pair, d_pair, s_row, d_row, s_in, d_in, attended, carried_q,
    gate_own, gate_in, norm_own, norm_in,
    gat, oacc, gradf, gbuf, xr, zf, zbuf, zr, out_v, grad_v,
    in_sem, w_sem, out_sem, a_send, a_recv, f_send, f_recv, r_sem, e_send, e_recv, s_send, s_recv, d_send, d_recv,
    gate_sem, norm_sem, g_send, g_recv, x_send, x_recv, z_sem,
):
    T = lax.axis_index("tm")
    M = lax.axis_index("mp")
    x, z = T // NZ, lax.rem(T, NZ)
    y, core = M // 2, lax.rem(M, 2)
    span, place = T // CH, lax.rem(T, CH)
    half_row = lax.rem(span, 2)
    at_home = lax.rem(span + 2 * x, CH) == place

    def held(at):
        return lax.rem(at + CH - 2 * x, CH)

    char = held(place)

    def holder(other_span, other_char):
        return other_span * CH + lax.rem(other_char + 2 * (other_span // 2), CH)

    right_y, left_y, opp_y = lax.rem(y + 1, NY), lax.rem(y + 3, NY), lax.rem(y + 2, NY)

    def load(src, dst, i):
        return pltpu.make_async_copy(src, dst, in_sem.at[i])

    loads = [
        load(resets, res_v, 0), load(contact, con_v, 1), load(bias, bias_v, 2),
        load(gain, gain_v, 3), load(ow, ow_v, 4), load(cot, cot_v, 5),
    ]
    loads[0].start()

    barrier = pltpu.get_barrier_semaphore()

    @pl.loop(1, TM)
    def _(k):
        pl.semaphore_signal(barrier, inc=1, device_id=(lax.rem(T + k, TM), M), device_id_type=MESH)

    sib = 2 * y + 1 - core
    right, left, opp = 2 * right_y + core, 2 * left_y + core, 2 * opp_y + core
    for other in (sib, right, left):
        pl.semaphore_signal(barrier, inc=1, device_id=(T, other), device_id_type=MESH)

    for one in loads[1:]:
        one.start()

    @pl.loop(0, MP)
    def _(m):
        for j, w in enumerate((wq, wk, wv, wd, wg)):
            pltpu.make_async_copy(w.at[:, m], w_v.at[m, :, :, pl.ds(j * 128, 128)], w_sem).start()

    loads[0].wait()
    res = res_v[...].astype(F32)
    res = jnp.concatenate([res, jnp.zeros_like(res)], 1)
    for c in range(CH):
        res_own[c] = res[c : c + 1]
    res_in[place] = res_own[char]

    pl.semaphore_wait(barrier, TM - 1 + 3)

    def piece(src, dst, sems, peer):
        return pltpu.make_async_remote_copy(
            src_ref=src, dst_ref=dst, send_sem=sems.at[0], recv_sem=sems.at[1],
            device_id=(peer, M), device_id_type=MESH,
        )

    def wait_bytes(ref, sem):
        pltpu.make_async_copy(ref, ref, sem).wait()

    def piece_of_wave(src, dst, send, recv, d, peer):
        return pltpu.make_async_remote_copy(
            src_ref=src, dst_ref=dst, send_sem=send, recv_sem=recv.at[d],
            device_id=(peer, M), device_id_type=MESH,
        )

    def quarter(to, d):
        return obs.at[:, pl.ds(pl.multiple_of(to * CH * FR + d * WAVE, WAVE), WAVE)]

    for d in range(NX):
        @pl.loop(0, CH)
        def _(k):
            to = lax.rem(span + k, CH)
            peer = holder(to, span)

            @pl.when(peer != T)
            def _():
                pltpu.make_async_remote_copy(
                    src_ref=quarter(to, d), dst_ref=rx.at[d, place], send_sem=a_send, recv_sem=a_recv.at[d],
                    device_id=(peer, M), device_id_type=MESH,
                ).start()

        @pl.when(at_home)
        def _():
            pltpu.make_async_copy(quarter(span, d), rx.at[d, place], a_recv.at[d]).start()

    @pl.loop(1, CH)
    def _(k):
        to = lax.rem(place + k, CH)
        piece(res_own.at[held(to)], res_in.at[place], r_sem, span * CH + to).start()

    for one in loads[1:]:
        one.wait()
    tri = (iota((FR, FR), 0) >= iota((FR, FR), 1)).astype(BF)
    wait_bytes(res_in.at[pl.ds(0, CH - 1)], r_sem.at[1])
    res = res_in[...].reshape(CH, 128)[:, :FR].astype(BF)
    seen_col = dot(tri, res, ((1,), (1,)))
    seen_row = dot(res, tri, ((1,), (1,)))
    for c in range(CH):
        rcol[c] = jnp.broadcast_to(seen_col[:, c : c + 1], (FR, 128))
        rrow[c] = seen_row[c : c + 1, :]
    t_id, s_id = iota((FR, FR), 0), iota((FR, FR), 1)
    for i, h in enumerate(LEVELS):
        masks[i] = ((t_id // (2 * h) == s_id // (2 * h)) & (t_id // h > s_id // h)).astype(F32)
        sel[i * FR : (i + 1) * FR] = (s_id == (t_id // (2 * h)) * (2 * h) + h - 1).astype(BF)
    masks[len(LEVELS)] = (t_id == s_id).astype(F32)

    row_q, col_q = iota((ROWS, FR), 0), iota((ROWS, FR), 1)
    pick = (((row_q % FR) // 8) * 8 + row_q // FR == col_q).astype(BF)
    con = con_v[...].astype(F32).astype(BF)
    taken = dot(pick, con).astype(BF)
    inv_partners[...] = 1.0 / jnp.maximum(dot(taken, jnp.ones((CH, 128), BF)), 1.0)
    spread = (iota((CH, ROWS), 1) // FR == iota((CH, ROWS), 0)).astype(BF)
    same = iota((ROWS, ROWS), 0) % FR == iota((ROWS, ROWS), 1) % FR
    @pl.loop(0, NX)
    def _(k):
        @pl.when(k >= x)
        def _():
            s_in[k] = jnp.zeros((128, 128), BF)
            d_in[k] = jnp.ones((1, 128), F32)

    mix[...] = jnp.where(same, dot(taken, spread), 0.0).astype(BF)

    bias_row, gain_row = bias_v[...], gain_v[...]
    pending = []

    def send(one):
        one.start()
        pending.append(one)

    def wave_rows(d):
        return pl.ds(d * WAVE, WAVE)

    def part(d, slot, i, to):
        ref = feat.at[slot, wave_rows(d)]
        return pltpu.make_async_remote_copy(
            src_ref=ref, dst_ref=ref, send_sem=f_send.at[d, i], recv_sem=f_recv.at[d, i],
            device_id=(T, to), device_id_type=MESH,
        )

    def own_features(d):
        wait_bytes(rx.at[d], a_recv.at[d])
        feat[M, wave_rows(d)] = rx[d].reshape(256, WAVE).T
        send(part(d, M, 1, right))
        send(part(d, M, 2, left))
        send(part(d, M, 0, sib))

    def pass_on(d):
        for slot, i, to in ((left, 1, right), (right, 2, left)) if d % 2 == 0 else ((right, 2, left), (left, 1, right)):
            part(d, slot, i, sib).wait_recv()
            if (i == 1) == (d % 2 == 0):
                send(part(d, slot, 3, to))
            send(part(d, slot, 3 + i, sib))

    def pass_opposite(d):
        part(d, opp, 3, sib).wait_recv()
        send(part(d, opp, 6, sib))

    wait_bytes(w_v, w_sem)

    def add_projections(d, slots, first):
        rows = wave_rows(d)
        total = None if first else proj[rows, :]
        for slot in slots:
            term = dot(feat[slot, rows], w_v[slot].reshape(256, 640))
            total = term if total is None else total + term
        proj[rows, :] = total

    def project(d):
        part(d, sib, 0, sib).wait_recv()
        add_projections(d, (M, left, right, opp, sib), True)
        others = [2 * yy + 1 - core for yy in (left_y, right_y, opp_y)]
        for slot, i in zip(others, (4, 5, 6)):
            part(d, slot, i, sib).wait_recv()
        add_projections(d, others, False)

    def states(d):
        for s in (2 * d, 2 * d + 1):
            rows = pl.ds(s * FR, FR)
            logit = proj[rows, 384:512] + bias_row
            u = jnp.exp(-jnp.abs(logit))
            log1p = jnp.where(u < 1e-3, u * (1.0 - 0.5 * u), jnp.log(1.0 + u))
            log_decay = jnp.minimum(logit, 0.0) - log1p
            both = dot(tri, jnp.concatenate(split(log_decay), 1))
            total = both[:, :128] + both[:, 128:]
            decay_log[rows, :] = total
            seen = rcol[s]
            last, last_seen = total[FR - 1 :], seen[FR - 1 :]
            weight = jnp.where(seen == last_seen, jnp.exp(jnp.minimum(last - total, 0.0)), 0.0)
            state = dot3(proj[rows, 128:256] * weight, proj[rows, 256:384], ((0,), (0,)))
            decay = jnp.where(last_seen == 0.0, jnp.exp(last), 0.0)
            if s == 0:
                before[0] = jnp.ones((1, 128), F32)
                local_state[0] = jnp.zeros((128, 128), F32)
                after, product = state, decay
            else:
                after = local_state[s] * column(decay) + state
                product = before[s] * decay
            if s < CH - 1:
                local_state[s + 1] = after
                before[s + 1] = product
            else:
                s_last[...] = after
                s_own[...] = after.astype(BF)
                d_own[...] = product

    def gates(d):
        gate = proj[wave_rows(d), 512:640]
        gate_own[wave_rows(d)] = (gate / (1.0 + jnp.exp(-gate))).astype(BF)
        for s in (2 * d, 2 * d + 1):
            @pl.when(s != place)
            def _():
                piece(gate_own.at[pl.ds(s * FR, FR)], gate_in.at[char], gate_sem, span * CH + s).start()

    own_features(0)
    own_features(1)
    own_features(2)
    pass_on(0)
    own_features(3)
    pass_on(1)
    pass_opposite(0)
    pass_on(2)
    pass_opposite(1)
    pass_on(3)
    pass_opposite(2)
    project(0)
    gates(0)
    pass_opposite(3)
    project(1)
    gates(1)
    states(0)
    project(2)
    gates(2)
    states(1)
    states(2)
    project(3)
    states(3)

    def inside(low, high):
        @pl.loop(low, high)
        def _(c):
            inside_one(c)

    def inside_one(c):
        rows = pl.ds(pl.multiple_of(c * FR, FR), FR)
        total = decay_log[rows, :]
        queries = proj[rows, 0:128] * HK ** (-0.5)
        keys, values = proj[rows, 128:256], proj[rows, 256:384]
        seen = rcol[c]
        carried = jnp.where(seen == 0.0, queries * jnp.exp(total), 0.0)
        carried_q[rows, :] = carried * before[c]
        picked = dot(sel[...], jnp.concatenate(split(total), 1))
        picked = picked[:, :128] + picked[:, 128:]
        scores = masks[len(LEVELS)] * dot3(queries, keys, ((1,), (1,)))
        for i in range(len(LEVELS)):
            gap = jnp.exp(-jnp.abs(total - picked[i * FR : (i + 1) * FR]))
            scores += masks[i] * dot3(queries * gap, keys * gap, ((1,), (1,)))
        scores = jnp.where(seen[:, :FR] == rrow[c], scores, 0.0)
        attended[rows, :] = dot3(scores, values) + dot3(carried, local_state[c])

    def exchange(i, src, dst, peer):
        return pltpu.make_async_remote_copy(
            src_ref=src, dst_ref=dst, send_sem=e_send.at[i], recv_sem=e_recv.at[i],
            device_id=(peer, M), device_id_type=MESH,
        )

    other = holder(span + 1 - 2 * half_row, char)
    swap = [exchange(0, s_own, s_pair, other), exchange(1, d_own, d_pair, other)]
    for one in swap:
        one.start()

    gates(3)
    gate_in[char] = gate_own[pl.ds(pl.multiple_of(place * FR, FR), FR)]
    inside(0, 6)

    def to_owners(src, dst, sems):
        @pl.loop(1, CH)
        def _(k):
            to = lax.rem(place + k, CH)
            rows = pl.ds(pl.multiple_of(to * FR, FR), FR)
            piece(src.at[rows], dst.at[char], sems, span * CH + to).start()

        dst[char] = src[pl.ds(pl.multiple_of(place * FR, FR), FR)]

    for one in swap:
        one.wait_recv()
    upper = half_row == 1
    mine, theirs = s_last[...], s_pair[...].astype(F32)
    my_decay, their_decay = d_own[...], d_pair[...]
    late_decay = column(jnp.where(upper, my_decay, their_decay))
    s_row[...] = (late_decay * jnp.where(upper, theirs, mine) + jnp.where(upper, mine, theirs)).astype(BF)
    d_row[...] = my_decay * their_decay

    def to_row(k):
        peer = holder(lax.rem(span + 2 * k, CH), char)
        return [
            pltpu.make_async_remote_copy(
                src_ref=src, dst_ref=dst.at[x], send_sem=sent.at[k], recv_sem=recv.at[x],
                device_id=(peer, M), device_id_type=MESH,
            )
            for src, dst, sent, recv in ((s_row, s_in, s_send, s_recv), (d_row, d_in, d_send, d_recv))
        ]

    for k in range(1, NX):
        @pl.when(x + k < NX)
        def _():
            for one in to_row(k):
                one.start()


    inside(6, CH)

    for k in range(NX - 1):
        @pl.when(k < x)
        def _():
            pltpu.make_async_copy(s_in.at[k], s_in.at[k], s_recv.at[k]).wait()
            pltpu.make_async_copy(d_in.at[k], d_in.at[k], d_recv.at[k]).wait()

    state = s_in[0].astype(F32)
    for k in range(1, NX - 1):
        state = state * column(d_in[k]) + s_in[k].astype(F32)
    state = jnp.where(upper, state * column(d_pair[...]) + s_pair[...].astype(F32), state)
    full = attended[...] + dot3(carried_q[...], state)
    square = jnp.mean(full * full, axis=-1, keepdims=True)
    norm_own[...] = (full * lax.rsqrt(square + 1e-06) * gain_row).astype(BF)
    to_owners(norm_own, norm_in, norm_sem)
    wait_bytes(gate_in.at[pl.ds(0, CH - 1)], gate_sem.at[1])
    silu = gate_in[...].reshape(ROWS, 128).astype(F32)
    wait_bytes(norm_in.at[pl.ds(0, CH - 1)], norm_sem.at[1])
    normed = norm_in[...].reshape(ROWS, 128).astype(F32)
    mixed = dot(mix[...], norm_in[...].reshape(ROWS, 128))
    gat[M] = ((normed + mixed * inv_partners[...]) * silu).astype(BF)

    half = ROWS // 2

    def gated_part(slot, h, i, to):
        ref = gat.at[slot, pl.ds(h * half, half)]
        return pltpu.make_async_remote_copy(
            src_ref=ref, dst_ref=ref, send_sem=g_send.at[i], recv_sem=g_recv.at[i],
            device_id=(T, to), device_id_type=MESH,
        )

    def go(*args):
        send(gated_part(*args))

    def arrived(slot, h, i):
        gated_part(slot, h, i, sib).wait_recv()

    def along_x(m):
        to, j = m // 2, lax.rem(m, 2)
        return pltpu.make_async_remote_copy(
            src_ref=gbuf.at[m], dst_ref=xr.at[j, x], send_sem=x_send, recv_sem=x_recv.at[j],
            device_id=(to * NZ + z, M), device_id_type=MESH,
        )

    def produce(m, first=False):
        rows = gat[m]
        part = dot(rows, cot_v[...], ((0,), (0,))).reshape(8, 16, 256)
        gradf[m] = part
        gbuf[m] = part.astype(BF)

        @pl.when(m // 2 != x)
        def _():
            along_x(m).start()

        term = dot(rows, ow_v[m])
        oacc[...] = term if first else oacc[...] + term

    go(M, 0, 2, right)
    go(M, 1, 5, left)
    go(M, 0, 0, sib)
    go(M, 1, 1, sib)
    go(M, 1, 3, right)
    go(M, 0, 4, left)
    produce(M, True)
    arrived(left, 0, 2)
    go(left, 0, 6, right)
    go(left, 0, 8, sib)
    arrived(right, 1, 5)
    go(right, 1, 7, left)
    go(right, 1, 11, sib)
    arrived(sib, 0, 0)
    arrived(sib, 1, 1)
    arrived(left, 1, 3)
    go(left, 1, 9, sib)
    arrived(right, 0, 4)
    go(right, 0, 10, sib)
    produce(left)
    produce(right)
    arrived(opp, 0, 6)
    go(opp, 0, 12, sib)
    arrived(opp, 1, 7)
    go(opp, 1, 13, sib)
    produce(opp)
    produce(sib)
    for yy, i in ((left_y, 8), (right_y, 10), (opp_y, 12)):
        slot = 2 * yy + 1 - core
        arrived(slot, 0, i)
        arrived(slot, 1, i + 1)
        produce(slot)

    out_v[...] = oacc[...].astype(BF)
    store = pltpu.make_async_copy(out_v, out, out_sem.at[0])
    store.start()

    for j in (core, 1 - core):
        wait_bytes(xr.at[j, pl.ds(0, NX - 1)], x_recv.at[j])
        total = gradf[2 * x + j]
        for d in range(1, NX):
            total += xr[j, lax.rem(x + d, NX)].astype(F32)
        owners = pl.ds(j * 8, 8)
        zf[owners] = total
        zbuf[owners] = total.astype(BF)

        @pl.loop(0, 8)
        def _(k):
            to = j * 8 + lax.rem(z + k, 8)

            @pl.when(to != z)
            def _():
                piece(zbuf.at[to], zr.at[z], z_sem, x * NZ + to).start()

    wait_bytes(zr.at[pl.ds(0, NZ - 1)], z_sem.at[1])
    total = zf[z]
    for k in range(1, NZ):
        total += zr[lax.rem(z + k, NZ)].astype(F32)
    grad_v[...] = total
    last_store = pltpu.make_async_copy(grad_v, grad, out_sem.at[1])
    last_store.start()

    for d in range(NX):
        @pl.when(at_home)
        def _():
            wait_bytes(rx.at[d, pl.ds(0, CH - 1)], a_send)

        @pl.when(jnp.logical_not(at_home))
        def _():
            wait_bytes(rx.at[d], a_send)

    wait_bytes(res_in.at[pl.ds(0, CH - 1)], r_sem.at[0])
    for one in pending:
        one.wait_send()
    for one in swap:
        one.wait_send()
    for k in range(1, NX):
        @pl.when(x + k < NX)
        def _():
            for one in to_row(k):
                one.wait_send()

    wait_bytes(gate_in.at[pl.ds(0, CH - 1)], gate_sem.at[0])
    wait_bytes(norm_in.at[pl.ds(0, CH - 1)], norm_sem.at[0])
    for j in range(2):
        wait_bytes(xr.at[j, pl.ds(0, NX - 1)], x_send)
    wait_bytes(zbuf.at[pl.ds(0, NZ - 1)], z_sem.at[0])
    store.wait()
    last_store.wait()


def local(
    observations, contact, resets, q_weight, k_weight, v_weight, decay_weight, gate_weight,
    decay_bias, norm_gain, out_weight, out_cotangent,
):
    features = jnp.swapaxes(observations[0], 0, 1)
    weights = [
        w.reshape(8, MP, 32, 128) for w in (q_weight, k_weight, v_weight, decay_weight, gate_weight)
    ]
    vm = pltpu.VMEM
    dma = pltpu.SemaphoreType.DMA
    scratch = [
        vm((FR, CH), jnp.int32), vm((CH, FR), jnp.int32), vm((MP, 8, 32, 640), BF), vm((1, 128), F32),
        vm((1, 128), F32), vm((MP, 128, 256), BF), vm((ROWS, 256), BF),
        vm((NX, CH, 32, WAVE), BF), vm((MP, ROWS, 256), BF), vm((ROWS, 640), F32), vm((ROWS, 128), F32),
        vm((CH, 1, 128), F32), vm((CH, 1, 128), F32), vm((CH, FR, 128), F32), vm((CH, 1, FR), F32),
        vm((len(LEVELS) + 1, FR, FR), F32), vm((len(LEVELS) * FR, FR), BF),
        vm((ROWS, ROWS), BF), vm((ROWS, 128), F32),
        vm((CH, 128, 128), F32), vm((CH, 1, 128), F32), vm((128, 128), F32),
        vm((128, 128), BF), vm((1, 128), F32), vm((128, 128), BF), vm((1, 128), F32),
        vm((128, 128), BF), vm((1, 128), F32), vm((NX, 128, 128), BF), vm((NX, 1, 128), F32), vm((ROWS, 128), F32), vm((ROWS, 128), F32),
        vm((ROWS, 128), BF), vm((CH, FR, 128), BF), vm((ROWS, 128), BF), vm((CH, FR, 128), BF),
        vm((MP, ROWS, 128), BF), vm((ROWS, 256), F32), vm((MP, 8, 16, 256), F32),
        vm((MP, 8, 16, 256), BF), vm((2, NX, 8, 16, 256), BF), vm((NZ, 16, 256), F32),
        vm((NZ, 16, 256), BF), vm((NZ, 16, 256), BF), vm((ROWS, 256), BF), vm((16, 256), F32),
        dma((6,)), dma, dma((2,)), dma, dma((NX,)), dma((NX, 7)), dma((NX, 7)), dma((2,)),
        dma((2,)), dma((2,)), dma((NX,)), dma((NX,)), dma((NX,)), dma((NX,)), dma((2,)), dma((2,)), dma((14,)), dma((14,)), dma, dma((2,)), dma((2,)),
    ]
    following, weight_grad = pl.pallas_call(
        kernel,
        out_shape=(
            jax.ShapeDtypeStruct((ROWS, 256), BF),
            jax.ShapeDtypeStruct((16, 256), F32),
        ),
        in_specs=[pl.BlockSpec(memory_space=pltpu.HBM)] * 12,
        out_specs=(pl.BlockSpec(memory_space=pltpu.HBM),) * 2,
        scratch_shapes=scratch,
        compiler_params=pltpu.CompilerParams(
            collective_id=0, has_side_effects=True, vmem_limit_bytes=60 * 2**20
        ),
    )(
        features, contact.reshape(FR, CH), resets, *weights, decay_bias, norm_gain,
        out_weight.reshape(MP, 128, 256), out_cotangent.reshape(ROWS, 256),
    )
    return following.reshape(CH, FR, 256), weight_grad


def solution(mesh):
    placed = (
        P("tm", None, "mp"),
        P("tm", None, None),
        P(None, "tm"),
        P(None, "mp"),
        P(None, "mp"),
        P(None, "mp"),
        P(None, "mp"),
        P(None, "mp"),
        P("mp", None),
        P("mp", None),
        P(None, "mp"),
        P(None, "tm", "mp"),
    )
    return jax.shard_map(
        local,
        mesh=mesh,
        in_specs=placed,
        out_specs=(P(None, "tm", "mp"), P("tm", "mp")),
        check_vma=False,
    )
```

```python
import jax
import jax.numpy as jnp
from jax import lax
from jax.experimental import pallas as pl
from jax.experimental.pallas import tpu as pltpu
from jax.sharding import PartitionSpec as P

MESH = pl.DeviceIdType.MESH
BF = jnp.bfloat16
F32 = jnp.float32

HK = 128
CH = 8
TM, MP = 64, 8
NX, NZ, NY = 4, 16, 4
FR = 64
ROWS = CH * FR
LEVELS = (32, 16, 8, 4, 2, 1)
WAVE = 2 * FR


def dot(a, b, dims=((1,), (0,))):
    return lax.dot_general(a, b, (dims, ((), ())), preferred_element_type=F32)


def split(a):
    high = a.astype(BF)
    return high, (a - high.astype(F32)).astype(BF)


def dot3(a, b, dims=((1,), (0,))):
    ah, al = split(a)
    bh, bl = split(b)
    da, db = dims[0][0], dims[1][0]
    return dot(jnp.concatenate([ah, al, ah], da), jnp.concatenate([bh, bh, bl], db), dims)


def iota(shape, dim):
    return lax.broadcasted_iota(jnp.int32, shape, dim)


def column(row):
    return jnp.broadcast_to(row, (8, 128)).T[:, :1]


def kernel(
    obs, contact, resets, wq, wk, wv, wd, wg, bias, gain, ow, cot,
    out, grad,
    con_v, res_v, w_v, bias_v, gain_v, ow_v, cot_v,
    rx, feat, proj, decay_log, res_own, res_in, rcol, rrow, masks, sel, mix, inv_partners,
    local_state, before, s_last, s_own, d_own, s_pair, d_pair, s_row, d_row, s_in, d_in, attended, carried_q,
    gate_own, gate_in, norm_own, norm_in,
    gat, oacc, gradf, gbuf, xr, zf, zbuf, zr, out_v, grad_v,
    in_sem, w_sem, out_sem, a_send, a_recv, f_send, f_recv, r_sem, e_send, e_recv, s_send, s_recv, d_send, d_recv,
    gate_sem, norm_sem, g_send, g_recv, x_send, x_recv, z_sem,
):
    T = lax.axis_index("tm")
    M = lax.axis_index("mp")
    x, z = T // NZ, lax.rem(T, NZ)
    y, core = M // 2, lax.rem(M, 2)
    span, place = T // CH, lax.rem(T, CH)
    half_row = lax.rem(span, 2)
    at_home = lax.rem(span + 2 * x, CH) == place

    def held(at):
        return lax.rem(at + CH - 2 * x, CH)

    char = held(place)

    def holder(other_span, other_char):
        return other_span * CH + lax.rem(other_char + 2 * (other_span // 2), CH)

    right_y, left_y, opp_y = lax.rem(y + 1, NY), lax.rem(y + 3, NY), lax.rem(y + 2, NY)

    def load(src, dst, i):
        return pltpu.make_async_copy(src, dst, in_sem.at[i])

    loads = [
        load(resets, res_v, 0), load(contact, con_v, 1), load(bias, bias_v, 2),
        load(gain, gain_v, 3), load(ow, ow_v, 4), load(cot, cot_v, 5),
    ]
    loads[0].start()

    barrier = pltpu.get_barrier_semaphore()

    @pl.loop(1, TM)
    def _(k):
        pl.semaphore_signal(barrier, inc=1, device_id=(lax.rem(T + k, TM), M), device_id_type=MESH)

    sib = 2 * y + 1 - core
    right, left, opp = 2 * right_y + core, 2 * left_y + core, 2 * opp_y + core
    for other in (sib, right, left):
        pl.semaphore_signal(barrier, inc=1, device_id=(T, other), device_id_type=MESH)

    for one in loads[1:]:
        one.start()

    @pl.loop(0, MP)
    def _(m):
        for j, w in enumerate((wq, wk, wv, wd, wg)):
            pltpu.make_async_copy(w.at[:, m], w_v.at[m, :, :, pl.ds(j * 128, 128)], w_sem).start()

    loads[0].wait()
    res = res_v[...].astype(F32)
    res = jnp.concatenate([res, jnp.zeros_like(res)], 1)
    for c in range(CH):
        res_own[c] = res[c : c + 1]
    res_in[place] = res_own[char]

    pl.semaphore_wait(barrier, TM - 1 + 3)

    def piece(src, dst, sems, peer):
        return pltpu.make_async_remote_copy(
            src_ref=src, dst_ref=dst, send_sem=sems.at[0], recv_sem=sems.at[1],
            device_id=(peer, M), device_id_type=MESH,
        )

    def wait_bytes(ref, sem):
        pltpu.make_async_copy(ref, ref, sem).wait()

    def piece_of_wave(src, dst, send, recv, d, peer):
        return pltpu.make_async_remote_copy(
            src_ref=src, dst_ref=dst, send_sem=send, recv_sem=recv.at[d],
            device_id=(peer, M), device_id_type=MESH,
        )

    def quarter(to, d):
        return obs.at[:, pl.ds(pl.multiple_of(to * CH * FR + d * WAVE, WAVE), WAVE)]

    for d in range(NX):
        @pl.loop(0, CH)
        def _(k):
            to = lax.rem(span + k, CH)
            peer = holder(to, span)

            @pl.when(peer != T)
            def _():
                pltpu.make_async_remote_copy(
                    src_ref=quarter(to, d), dst_ref=rx.at[d, place], send_sem=a_send, recv_sem=a_recv.at[d],
                    device_id=(peer, M), device_id_type=MESH,
                ).start()

        @pl.when(at_home)
        def _():
            pltpu.make_async_copy(quarter(span, d), rx.at[d, place], a_recv.at[d]).start()

    @pl.loop(1, CH)
    def _(k):
        to = lax.rem(place + k, CH)
        piece(res_own.at[held(to)], res_in.at[place], r_sem, span * CH + to).start()

    for one in loads[1:]:
        one.wait()
    tri = (iota((FR, FR), 0) >= iota((FR, FR), 1)).astype(BF)
    wait_bytes(res_in.at[pl.ds(0, CH - 1)], r_sem.at[1])
    res = res_in[...].reshape(CH, 128)[:, :FR].astype(BF)
    seen_col = dot(tri, res, ((1,), (1,)))
    seen_row = dot(res, tri, ((1,), (1,)))
    for c in range(CH):
        rcol[c] = jnp.broadcast_to(seen_col[:, c : c + 1], (FR, 128))
        rrow[c] = seen_row[c : c + 1, :]
    t_id, s_id = iota((FR, FR), 0), iota((FR, FR), 1)
    for i, h in enumerate(LEVELS):
        masks[i] = ((t_id // (2 * h) == s_id // (2 * h)) & (t_id // h > s_id // h)).astype(F32)
        sel[i * FR : (i + 1) * FR] = (s_id == (t_id // (2 * h)) * (2 * h) + h - 1).astype(BF)
    masks[len(LEVELS)] = (t_id == s_id).astype(F32)

    row_q, col_q = iota((ROWS, FR), 0), iota((ROWS, FR), 1)
    pick = (((row_q % FR) // 8) * 8 + row_q // FR == col_q).astype(BF)
    con = con_v[...].astype(F32).astype(BF)
    taken = dot(pick, con).astype(BF)
    inv_partners[...] = 1.0 / jnp.maximum(dot(taken, jnp.ones((CH, 128), BF)), 1.0)
    spread = (iota((CH, ROWS), 1) // FR == iota((CH, ROWS), 0)).astype(BF)
    same = iota((ROWS, ROWS), 0) % FR == iota((ROWS, ROWS), 1) % FR
    @pl.loop(0, NX)
    def _(k):
        @pl.when(k >= x)
        def _():
            s_in[k] = jnp.zeros((128, 128), BF)
            d_in[k] = jnp.ones((1, 128), F32)

    mix[...] = jnp.where(same, dot(taken, spread), 0.0).astype(BF)

    bias_row, gain_row = bias_v[...], gain_v[...]
    pending = []

    def send(one):
        one.start()
        pending.append(one)

    def wave_rows(d):
        return pl.ds(d * WAVE, WAVE)

    def part(d, slot, i, to):
        ref = feat.at[slot, wave_rows(d)]
        return pltpu.make_async_remote_copy(
            src_ref=ref, dst_ref=ref, send_sem=f_send.at[d, i], recv_sem=f_recv.at[d, i],
            device_id=(T, to), device_id_type=MESH,
        )

    def own_features(d):
        wait_bytes(rx.at[d], a_recv.at[d])
        feat[M, wave_rows(d)] = rx[d].reshape(256, WAVE).T
        send(part(d, M, 1, right))
        send(part(d, M, 2, left))
        send(part(d, M, 0, sib))

    def pass_on(d):
        for slot, i, to in ((left, 1, right), (right, 2, left)) if d % 2 == 0 else ((right, 2, left), (left, 1, right)):
            part(d, slot, i, sib).wait_recv()
            if (i == 1) == (d % 2 == 0):
                send(part(d, slot, 3, to))
            send(part(d, slot, 3 + i, sib))

    def pass_opposite(d):
        part(d, opp, 3, sib).wait_recv()
        send(part(d, opp, 6, sib))

    wait_bytes(w_v, w_sem)

    def add_projections(d, slots, first):
        rows = wave_rows(d)
        total = None if first else proj[rows, :]
        for slot in slots:
            term = dot(feat[slot, rows], w_v[slot].reshape(256, 640))
            total = term if total is None else total + term
        proj[rows, :] = total

    def project(d):
        part(d, sib, 0, sib).wait_recv()
        add_projections(d, (M, left, right, opp, sib), True)
        others = [2 * yy + 1 - core for yy in (left_y, right_y, opp_y)]
        for slot, i in zip(others, (4, 5, 6)):
            part(d, slot, i, sib).wait_recv()
        add_projections(d, others, False)

    def states(d):
        for s in (2 * d, 2 * d + 1):
            rows = pl.ds(s * FR, FR)
            logit = proj[rows, 384:512] + bias_row
            u = jnp.exp(-jnp.abs(logit))
            log1p = jnp.where(u < 1e-3, u * (1.0 - 0.5 * u), jnp.log(1.0 + u))
            log_decay = jnp.minimum(logit, 0.0) - log1p
            both = dot(tri, jnp.concatenate(split(log_decay), 1))
            total = both[:, :128] + both[:, 128:]
            decay_log[rows, :] = total
            seen = rcol[s]
            last, last_seen = total[FR - 1 :], seen[FR - 1 :]
            weight = jnp.where(seen == last_seen, jnp.exp(jnp.minimum(last - total, 0.0)), 0.0)
            state = dot3(proj[rows, 128:256] * weight, proj[rows, 256:384], ((0,), (0,)))
            decay = jnp.where(last_seen == 0.0, jnp.exp(last), 0.0)
            if s == 0:
                before[0] = jnp.ones((1, 128), F32)
                local_state[0] = jnp.zeros((128, 128), F32)
                after, product = state, decay
            else:
                after = local_state[s] * column(decay) + state
                product = before[s] * decay
            if s < CH - 1:
                local_state[s + 1] = after
                before[s + 1] = product
            else:
                s_last[...] = after
                s_own[...] = after.astype(BF)
                d_own[...] = product

    def gates(d):
        gate = proj[wave_rows(d), 512:640]
        gate_own[wave_rows(d)] = (gate / (1.0 + jnp.exp(-gate))).astype(BF)
        for s in (2 * d, 2 * d + 1):
            @pl.when(s != place)
            def _():
                piece(gate_own.at[pl.ds(s * FR, FR)], gate_in.at[char], gate_sem, span * CH + s).start()

    own_features(0)
    own_features(1)
    own_features(2)
    pass_on(0)
    own_features(3)
    pass_on(1)
    pass_opposite(0)
    pass_on(2)
    pass_opposite(1)
    pass_on(3)
    pass_opposite(2)
    project(0)
    gates(0)
    pass_opposite(3)
    project(1)
    gates(1)
    states(0)
    project(2)
    gates(2)
    states(1)
    states(2)
    project(3)
    states(3)

    def inside(low, high):
        @pl.loop(low, high)
        def _(c):
            inside_one(c)

    def inside_one(c):
        rows = pl.ds(pl.multiple_of(c * FR, FR), FR)
        total = decay_log[rows, :]
        queries = proj[rows, 0:128] * HK ** (-0.5)
        keys, values = proj[rows, 128:256], proj[rows, 256:384]
        seen = rcol[c]
        carried = jnp.where(seen == 0.0, queries * jnp.exp(total), 0.0)
        carried_q[rows, :] = carried * before[c]
        picked = dot(sel[...], jnp.concatenate(split(total), 1))
        picked = picked[:, :128] + picked[:, 128:]
        scores = masks[len(LEVELS)] * dot3(queries, keys, ((1,), (1,)))
        for i in range(len(LEVELS)):
            gap = jnp.exp(-jnp.abs(total - picked[i * FR : (i + 1) * FR]))
            scores += masks[i] * dot3(queries * gap, keys * gap, ((1,), (1,)))
        scores = jnp.where(seen[:, :FR] == rrow[c], scores, 0.0)
        attended[rows, :] = dot3(scores, values) + dot3(carried, local_state[c])

    def exchange(i, src, dst, peer):
        return pltpu.make_async_remote_copy(
            src_ref=src, dst_ref=dst, send_sem=e_send.at[i], recv_sem=e_recv.at[i],
            device_id=(peer, M), device_id_type=MESH,
        )

    other = holder(span + 1 - 2 * half_row, char)
    swap = [exchange(0, s_own, s_pair, other), exchange(1, d_own, d_pair, other)]
    for one in swap:
        one.start()

    gates(3)
    gate_in[char] = gate_own[pl.ds(pl.multiple_of(place * FR, FR), FR)]
    inside(0, 6)

    def to_owners(src, dst, sems):
        @pl.loop(1, CH)
        def _(k):
            to = lax.rem(place + k, CH)
            rows = pl.ds(pl.multiple_of(to * FR, FR), FR)
            piece(src.at[rows], dst.at[char], sems, span * CH + to).start()

        dst[char] = src[pl.ds(pl.multiple_of(place * FR, FR), FR)]

    for one in swap:
        one.wait_recv()
    upper = half_row == 1
    mine, theirs = s_last[...], s_pair[...].astype(F32)
    my_decay, their_decay = d_own[...], d_pair[...]
    late_decay = column(jnp.where(upper, my_decay, their_decay))
    s_row[...] = (late_decay * jnp.where(upper, theirs, mine) + jnp.where(upper, mine, theirs)).astype(BF)
    d_row[...] = my_decay * their_decay

    def to_row(k):
        if k == 2:
            peer = holder(lax.rem(span + 4, CH), char)
        else:
            peer = lax.rem(x + k, NX) * NZ + lax.rem(z + (2 if k == 1 else NZ - 2), NZ)
        return [
            pltpu.make_async_remote_copy(
                src_ref=src, dst_ref=dst.at[x], send_sem=sent.at[k], recv_sem=recv.at[x],
                device_id=(peer, M), device_id_type=MESH,
            )
            for src, dst, sent, recv in ((s_row, s_in, s_send, s_recv), (d_row, d_in, d_send, d_recv))
        ]

    for k in range(1, NX):
        @pl.when(x + k < NX)
        def _():
            for one in to_row(k):
                one.start()


    inside(6, CH)

    for k in range(NX - 1):
        @pl.when(k < x)
        def _():
            pltpu.make_async_copy(s_in.at[k], s_in.at[k], s_recv.at[k]).wait()
            pltpu.make_async_copy(d_in.at[k], d_in.at[k], d_recv.at[k]).wait()

    state = s_in[0].astype(F32)
    for k in range(1, NX - 1):
        state = state * column(d_in[k]) + s_in[k].astype(F32)
    state = jnp.where(upper, state * column(d_pair[...]) + s_pair[...].astype(F32), state)
    full = attended[...] + dot3(carried_q[...], state)
    square = jnp.mean(full * full, axis=-1, keepdims=True)
    norm_own[...] = (full * lax.rsqrt(square + 1e-06) * gain_row).astype(BF)
    to_owners(norm_own, norm_in, norm_sem)
    wait_bytes(gate_in.at[pl.ds(0, CH - 1)], gate_sem.at[1])
    silu = gate_in[...].reshape(ROWS, 128).astype(F32)
    wait_bytes(norm_in.at[pl.ds(0, CH - 1)], norm_sem.at[1])
    normed = norm_in[...].reshape(ROWS, 128).astype(F32)
    mixed = dot(mix[...], norm_in[...].reshape(ROWS, 128))
    gat[M] = ((normed + mixed * inv_partners[...]) * silu).astype(BF)

    half = ROWS // 2

    def gated_part(slot, h, i, to):
        ref = gat.at[slot, pl.ds(h * half, half)]
        return pltpu.make_async_remote_copy(
            src_ref=ref, dst_ref=ref, send_sem=g_send.at[i], recv_sem=g_recv.at[i],
            device_id=(T, to), device_id_type=MESH,
        )

    def go(*args):
        send(gated_part(*args))

    def arrived(slot, h, i):
        gated_part(slot, h, i, sib).wait_recv()

    def along_x(m):
        to, j = m // 2, lax.rem(m, 2)
        return pltpu.make_async_remote_copy(
            src_ref=gbuf.at[m], dst_ref=xr.at[j, x], send_sem=x_send, recv_sem=x_recv.at[j],
            device_id=(to * NZ + z, M), device_id_type=MESH,
        )

    def produce(m, first=False):
        rows = gat[m]
        part = dot(rows, cot_v[...], ((0,), (0,))).reshape(8, 16, 256)
        gradf[m] = part
        gbuf[m] = part.astype(BF)

        @pl.when(m // 2 != x)
        def _():
            along_x(m).start()

        term = dot(rows, ow_v[m])
        oacc[...] = term if first else oacc[...] + term

    go(M, 0, 2, right)
    go(M, 1, 5, left)
    go(M, 0, 0, sib)
    go(M, 1, 1, sib)
    go(M, 1, 3, right)
    go(M, 0, 4, left)
    produce(M, True)
    arrived(left, 0, 2)
    go(left, 0, 6, right)
    go(left, 0, 8, sib)
    arrived(right, 1, 5)
    go(right, 1, 7, left)
    go(right, 1, 11, sib)
    arrived(sib, 0, 0)
    arrived(sib, 1, 1)
    arrived(left, 1, 3)
    go(left, 1, 9, sib)
    arrived(right, 0, 4)
    go(right, 0, 10, sib)
    produce(left)
    produce(right)
    arrived(opp, 0, 6)
    go(opp, 0, 12, sib)
    arrived(opp, 1, 7)
    go(opp, 1, 13, sib)
    produce(opp)
    produce(sib)
    for yy, i in ((left_y, 8), (right_y, 10), (opp_y, 12)):
        slot = 2 * yy + 1 - core
        arrived(slot, 0, i)
        arrived(slot, 1, i + 1)
        produce(slot)

    out_v[...] = oacc[...].astype(BF)
    store = pltpu.make_async_copy(out_v, out, out_sem.at[0])
    store.start()

    for j in (core, 1 - core):
        wait_bytes(xr.at[j, pl.ds(0, NX - 1)], x_recv.at[j])
        total = gradf[2 * x + j]
        for d in range(1, NX):
            total += xr[j, lax.rem(x + d, NX)].astype(F32)
        owners = pl.ds(j * 8, 8)
        zf[owners] = total
        zbuf[owners] = total.astype(BF)

        @pl.loop(0, 8)
        def _(k):
            to = j * 8 + lax.rem(z + k, 8)

            @pl.when(to != z)
            def _():
                piece(zbuf.at[to], zr.at[z], z_sem, x * NZ + to).start()

    wait_bytes(zr.at[pl.ds(0, NZ - 1)], z_sem.at[1])
    total = zf[z]
    for k in range(1, NZ):
        total += zr[lax.rem(z + k, NZ)].astype(F32)
    grad_v[...] = total
    last_store = pltpu.make_async_copy(grad_v, grad, out_sem.at[1])
    last_store.start()

    for d in range(NX):
        @pl.when(at_home)
        def _():
            wait_bytes(rx.at[d, pl.ds(0, CH - 1)], a_send)

        @pl.when(jnp.logical_not(at_home))
        def _():
            wait_bytes(rx.at[d], a_send)

    wait_bytes(res_in.at[pl.ds(0, CH - 1)], r_sem.at[0])
    for one in pending:
        one.wait_send()
    for one in swap:
        one.wait_send()
    for k in range(1, NX):
        @pl.when(x + k < NX)
        def _():
            for one in to_row(k):
                one.wait_send()

    wait_bytes(gate_in.at[pl.ds(0, CH - 1)], gate_sem.at[0])
    wait_bytes(norm_in.at[pl.ds(0, CH - 1)], norm_sem.at[0])
    for j in range(2):
        wait_bytes(xr.at[j, pl.ds(0, NX - 1)], x_send)
    wait_bytes(zbuf.at[pl.ds(0, NZ - 1)], z_sem.at[0])
    store.wait()
    last_store.wait()


def local(
    observations, contact, resets, q_weight, k_weight, v_weight, decay_weight, gate_weight,
    decay_bias, norm_gain, out_weight, out_cotangent,
):
    features = jnp.swapaxes(observations[0], 0, 1)
    weights = [
        w.reshape(8, MP, 32, 128) for w in (q_weight, k_weight, v_weight, decay_weight, gate_weight)
    ]
    vm = pltpu.VMEM
    dma = pltpu.SemaphoreType.DMA
    scratch = [
        vm((FR, CH), jnp.int32), vm((CH, FR), jnp.int32), vm((MP, 8, 32, 640), BF), vm((1, 128), F32),
        vm((1, 128), F32), vm((MP, 128, 256), BF), vm((ROWS, 256), BF),
        vm((NX, CH, 32, WAVE), BF), vm((MP, ROWS, 256), BF), vm((ROWS, 640), F32), vm((ROWS, 128), F32),
        vm((CH, 1, 128), F32), vm((CH, 1, 128), F32), vm((CH, FR, 128), F32), vm((CH, 1, FR), F32),
        vm((len(LEVELS) + 1, FR, FR), F32), vm((len(LEVELS) * FR, FR), BF),
        vm((ROWS, ROWS), BF), vm((ROWS, 128), F32),
        vm((CH, 128, 128), F32), vm((CH, 1, 128), F32), vm((128, 128), F32),
        vm((128, 128), BF), vm((1, 128), F32), vm((128, 128), BF), vm((1, 128), F32),
        vm((128, 128), BF), vm((1, 128), F32), vm((NX, 128, 128), BF), vm((NX, 1, 128), F32), vm((ROWS, 128), F32), vm((ROWS, 128), F32),
        vm((ROWS, 128), BF), vm((CH, FR, 128), BF), vm((ROWS, 128), BF), vm((CH, FR, 128), BF),
        vm((MP, ROWS, 128), BF), vm((ROWS, 256), F32), vm((MP, 8, 16, 256), F32),
        vm((MP, 8, 16, 256), BF), vm((2, NX, 8, 16, 256), BF), vm((NZ, 16, 256), F32),
        vm((NZ, 16, 256), BF), vm((NZ, 16, 256), BF), vm((ROWS, 256), BF), vm((16, 256), F32),
        dma((6,)), dma, dma((2,)), dma, dma((NX,)), dma((NX, 7)), dma((NX, 7)), dma((2,)),
        dma((2,)), dma((2,)), dma((NX,)), dma((NX,)), dma((NX,)), dma((NX,)), dma((2,)), dma((2,)), dma((14,)), dma((14,)), dma, dma((2,)), dma((2,)),
    ]
    following, weight_grad = pl.pallas_call(
        kernel,
        out_shape=(
            jax.ShapeDtypeStruct((ROWS, 256), BF),
            jax.ShapeDtypeStruct((16, 256), F32),
        ),
        in_specs=[pl.BlockSpec(memory_space=pltpu.HBM)] * 12,
        out_specs=(pl.BlockSpec(memory_space=pltpu.HBM),) * 2,
        scratch_shapes=scratch,
        compiler_params=pltpu.CompilerParams(
            collective_id=0, has_side_effects=True, vmem_limit_bytes=60 * 2**20
        ),
    )(
        features, contact.reshape(FR, CH), resets, *weights, decay_bias, norm_gain,
        out_weight.reshape(MP, 128, 256), out_cotangent.reshape(ROWS, 256),
    )
    return following.reshape(CH, FR, 256), weight_grad


def solution(mesh):
    placed = (
        P("tm", None, "mp"),
        P("tm", None, None),
        P(None, "tm"),
        P(None, "mp"),
        P(None, "mp"),
        P(None, "mp"),
        P(None, "mp"),
        P(None, "mp"),
        P("mp", None),
        P("mp", None),
        P(None, "mp"),
        P(None, "tm", "mp"),
    )
    return jax.shard_map(
        local,
        mesh=mesh,
        in_specs=placed,
        out_specs=(P(None, "tm", "mp"), P("tm", "mp")),
        check_vma=False,
    )
```

```python
import jax
import jax.numpy as jnp
from jax import lax
from jax.experimental import pallas as pl
from jax.experimental.pallas import tpu as pltpu
from jax.sharding import PartitionSpec as P

MESH = pl.DeviceIdType.MESH
BF = jnp.bfloat16
F32 = jnp.float32

HK = 128
CH = 8
TM, MP = 64, 8
NX, NZ, NY = 4, 16, 4
FR = 64
ROWS = CH * FR
LEVELS = (32, 16, 8, 4, 2, 1)
WAVE = 2 * FR


def dot(a, b, dims=((1,), (0,))):
    return lax.dot_general(a, b, (dims, ((), ())), preferred_element_type=F32)


def split(a):
    high = a.astype(BF)
    return high, (a - high.astype(F32)).astype(BF)


def dot3(a, b, dims=((1,), (0,))):
    ah, al = split(a)
    bh, bl = split(b)
    da, db = dims[0][0], dims[1][0]
    return dot(jnp.concatenate([ah, al, ah], da), jnp.concatenate([bh, bh, bl], db), dims)


def iota(shape, dim):
    return lax.broadcasted_iota(jnp.int32, shape, dim)


def column(row):
    return jnp.broadcast_to(row, (8, 128)).T[:, :1]


def kernel(
    obs, contact, resets, wq, wk, wv, wd, wg, bias, gain, ow, cot,
    out, grad,
    con_v, res_v, w_v, bias_v, gain_v, ow_v, cot_v,
    rx, feat, proj, decay_log, res_own, res_in, rcol, rrow, masks, sel, mix, inv_partners,
    local_state, before, s_last, s_own, d_own, s_pair, d_pair, s_row, d_row, s_in, d_in, attended, carried_q,
    gate_own, gate_in, norm_own, norm_in,
    gat, oacc, gradf, gbuf, xr, zf, zbuf, zr, out_v, grad_v,
    in_sem, w_sem, out_sem, a_send, a_recv, f_send, f_recv, r_sem, e_send, e_recv, s_send, s_recv, d_send, d_recv,
    gate_sem, norm_sem, g_send, g_recv, x_send, x_recv, z_sem,
):
    T = lax.axis_index("tm")
    M = lax.axis_index("mp")
    x, z = T // NZ, lax.rem(T, NZ)
    y, core = M // 2, lax.rem(M, 2)
    span, place = T // CH, lax.rem(T, CH)
    half_row = lax.rem(span, 2)
    at_home = lax.rem(span + 2 * x, CH) == place

    def held(at):
        return lax.rem(at + CH - 2 * x, CH)

    char = held(place)

    def holder(other_span, other_char):
        return other_span * CH + lax.rem(other_char + 2 * (other_span // 2), CH)

    right_y, left_y, opp_y = lax.rem(y + 1, NY), lax.rem(y + 3, NY), lax.rem(y + 2, NY)

    def load(src, dst, i):
        return pltpu.make_async_copy(src, dst, in_sem.at[i])

    loads = [
        load(resets, res_v, 0), load(contact, con_v, 1), load(bias, bias_v, 2),
        load(gain, gain_v, 3), load(ow, ow_v, 4), load(cot, cot_v, 5),
    ]
    loads[0].start()

    barrier = pltpu.get_barrier_semaphore()

    @pl.loop(1, TM)
    def _(k):
        pl.semaphore_signal(barrier, inc=1, device_id=(lax.rem(T + k, TM), M), device_id_type=MESH)

    sib = 2 * y + 1 - core
    right, left, opp = 2 * right_y + core, 2 * left_y + core, 2 * opp_y + core
    for other in (sib, right, left):
        pl.semaphore_signal(barrier, inc=1, device_id=(T, other), device_id_type=MESH)

    for one in loads[1:]:
        one.start()

    @pl.loop(0, MP)
    def _(m):
        for j, w in enumerate((wq, wk, wv, wd, wg)):
            pltpu.make_async_copy(w.at[:, m], w_v.at[m, :, :, pl.ds(j * 128, 128)], w_sem).start()

    loads[0].wait()
    res = res_v[...].astype(F32)
    res = jnp.concatenate([res, jnp.zeros_like(res)], 1)
    for c in range(CH):
        res_own[c] = res[c : c + 1]
    res_in[place] = res_own[char]

    pl.semaphore_wait(barrier, TM - 1 + 3)

    def piece(src, dst, sems, peer):
        return pltpu.make_async_remote_copy(
            src_ref=src, dst_ref=dst, send_sem=sems.at[0], recv_sem=sems.at[1],
            device_id=(peer, M), device_id_type=MESH,
        )

    def wait_bytes(ref, sem):
        pltpu.make_async_copy(ref, ref, sem).wait()

    def piece_of_wave(src, dst, send, recv, d, peer):
        return pltpu.make_async_remote_copy(
            src_ref=src, dst_ref=dst, send_sem=send, recv_sem=recv.at[d],
            device_id=(peer, M), device_id_type=MESH,
        )

    def quarter(to, d):
        return obs.at[:, pl.ds(pl.multiple_of(to * CH * FR + d * WAVE, WAVE), WAVE)]

    for d in range(NX):
        @pl.loop(0, CH)
        def _(k):
            to = lax.rem(span + k, CH)
            peer = holder(to, span)

            @pl.when(peer != T)
            def _():
                pltpu.make_async_remote_copy(
                    src_ref=quarter(to, d), dst_ref=rx.at[d, place], send_sem=a_send, recv_sem=a_recv.at[d],
                    device_id=(peer, M), device_id_type=MESH,
                ).start()

        @pl.when(at_home)
        def _():
            pltpu.make_async_copy(quarter(span, d), rx.at[d, place], a_recv.at[d]).start()

    @pl.loop(1, CH)
    def _(k):
        to = lax.rem(place + k, CH)
        piece(res_own.at[held(to)], res_in.at[place], r_sem, span * CH + to).start()

    for one in loads[1:]:
        one.wait()
    tri = (iota((FR, FR), 0) >= iota((FR, FR), 1)).astype(BF)
    wait_bytes(res_in.at[pl.ds(0, CH - 1)], r_sem.at[1])
    res = res_in[...].reshape(CH, 128)[:, :FR].astype(BF)
    seen_col = dot(tri, res, ((1,), (1,)))
    seen_row = dot(res, tri, ((1,), (1,)))
    for c in range(CH):
        rcol[c] = jnp.broadcast_to(seen_col[:, c : c + 1], (FR, 128))
        rrow[c] = seen_row[c : c + 1, :]
    t_id, s_id = iota((FR, FR), 0), iota((FR, FR), 1)
    for i, h in enumerate(LEVELS):
        masks[i] = ((t_id // (2 * h) == s_id // (2 * h)) & (t_id // h > s_id // h)).astype(F32)
        sel[i * FR : (i + 1) * FR] = (s_id == (t_id // (2 * h)) * (2 * h) + h - 1).astype(BF)
    masks[len(LEVELS)] = (t_id == s_id).astype(F32)

    row_q, col_q = iota((ROWS, FR), 0), iota((ROWS, FR), 1)
    pick = (((row_q % FR) // 8) * 8 + row_q // FR == col_q).astype(BF)
    con = con_v[...].astype(F32).astype(BF)
    taken = dot(pick, con).astype(BF)
    inv_partners[...] = 1.0 / jnp.maximum(dot(taken, jnp.ones((CH, 128), BF)), 1.0)
    spread = (iota((CH, ROWS), 1) // FR == iota((CH, ROWS), 0)).astype(BF)
    same = iota((ROWS, ROWS), 0) % FR == iota((ROWS, ROWS), 1) % FR
    @pl.loop(0, NX)
    def _(k):
        @pl.when(k >= x)
        def _():
            s_in[k] = jnp.zeros((128, 128), BF)
            d_in[k] = jnp.ones((1, 128), F32)

    mix[...] = jnp.where(same, dot(taken, spread), 0.0).astype(BF)

    bias_row, gain_row = bias_v[...], gain_v[...]
    pending = []

    def send(one):
        one.start()
        pending.append(one)

    def wave_rows(d):
        return pl.ds(d * WAVE, WAVE)

    def part(d, slot, i, to):
        ref = feat.at[slot, wave_rows(d)]
        return pltpu.make_async_remote_copy(
            src_ref=ref, dst_ref=ref, send_sem=f_send.at[d, i], recv_sem=f_recv.at[d, i],
            device_id=(T, to), device_id_type=MESH,
        )

    def own_features(d):
        wait_bytes(rx.at[d], a_recv.at[d])
        feat[M, wave_rows(d)] = rx[d].reshape(256, WAVE).T
        send(part(d, M, 1, right))
        send(part(d, M, 2, left))
        send(part(d, M, 0, sib))

    def pass_on(d):
        for slot, i, to in ((left, 1, right), (right, 2, left)) if d % 2 == 0 else ((right, 2, left), (left, 1, right)):
            part(d, slot, i, sib).wait_recv()
            if (i == 1) == (d % 2 == 0):
                send(part(d, slot, 3, to))
            send(part(d, slot, 3 + i, sib))

    def pass_opposite(d):
        part(d, opp, 3, sib).wait_recv()
        send(part(d, opp, 6, sib))

    wait_bytes(w_v, w_sem)

    def add_projections(d, slots, first):
        rows = wave_rows(d)
        total = None if first else proj[rows, :]
        for slot in slots:
            term = dot(feat[slot, rows], w_v[slot].reshape(256, 640))
            total = term if total is None else total + term
        proj[rows, :] = total

    def project(d):
        part(d, sib, 0, sib).wait_recv()
        add_projections(d, (M, left, right, opp, sib), True)
        others = [2 * yy + 1 - core for yy in (left_y, right_y, opp_y)]
        for slot, i in zip(others, (4, 5, 6)):
            part(d, slot, i, sib).wait_recv()
        add_projections(d, others, False)

    def states(d):
        for s in (2 * d, 2 * d + 1):
            rows = pl.ds(s * FR, FR)
            logit = proj[rows, 384:512] + bias_row
            u = jnp.exp(-jnp.abs(logit))
            log1p = jnp.where(u < 1e-3, u * (1.0 - 0.5 * u), jnp.log(1.0 + u))
            log_decay = jnp.minimum(logit, 0.0) - log1p
            both = dot(tri, jnp.concatenate(split(log_decay), 1))
            total = both[:, :128] + both[:, 128:]
            decay_log[rows, :] = total
            seen = rcol[s]
            last, last_seen = total[FR - 1 :], seen[FR - 1 :]
            weight = jnp.where(seen == last_seen, jnp.exp(jnp.minimum(last - total, 0.0)), 0.0)
            state = dot3(proj[rows, 128:256] * weight, proj[rows, 256:384], ((0,), (0,)))
            decay = jnp.where(last_seen == 0.0, jnp.exp(last), 0.0)
            if s == 0:
                before[0] = jnp.ones((1, 128), F32)
                local_state[0] = jnp.zeros((128, 128), F32)
                after, product = state, decay
            else:
                after = local_state[s] * column(decay) + state
                product = before[s] * decay
            if s < CH - 1:
                local_state[s + 1] = after
                before[s + 1] = product
            else:
                s_last[...] = after
                s_own[...] = after.astype(BF)
                d_own[...] = product

    def gates(d):
        gate = proj[wave_rows(d), 512:640]
        gate_own[wave_rows(d)] = (gate / (1.0 + jnp.exp(-gate))).astype(BF)
        for s in (2 * d, 2 * d + 1):
            @pl.when(s != place)
            def _():
                piece(gate_own.at[pl.ds(s * FR, FR)], gate_in.at[char], gate_sem, span * CH + s).start()

    own_features(0)
    own_features(1)
    own_features(2)
    pass_on(0)
    own_features(3)
    pass_on(1)
    pass_opposite(0)
    pass_on(2)
    pass_opposite(1)
    pass_on(3)
    pass_opposite(2)
    project(0)
    gates(0)
    pass_opposite(3)
    project(1)
    gates(1)
    states(0)
    project(2)
    gates(2)
    states(1)
    states(2)
    project(3)
    states(3)

    def inside(low, high):
        @pl.loop(low, high)
        def _(c):
            inside_one(c)

    def inside_one(c):
        rows = pl.ds(pl.multiple_of(c * FR, FR), FR)
        total = decay_log[rows, :]
        queries = proj[rows, 0:128] * HK ** (-0.5)
        keys, values = proj[rows, 128:256], proj[rows, 256:384]
        seen = rcol[c]
        carried = jnp.where(seen == 0.0, queries * jnp.exp(total), 0.0)
        carried_q[rows, :] = carried * before[c]
        picked = dot(sel[...], jnp.concatenate(split(total), 1))
        picked = picked[:, :128] + picked[:, 128:]
        scores = masks[len(LEVELS)] * dot3(queries, keys, ((1,), (1,)))
        for i in range(len(LEVELS)):
            gap = jnp.exp(-jnp.abs(total - picked[i * FR : (i + 1) * FR]))
            scores += masks[i] * dot3(queries * gap, keys * gap, ((1,), (1,)))
        scores = jnp.where(seen[:, :FR] == rrow[c], scores, 0.0)
        attended[rows, :] = dot3(scores, values) + dot3(carried, local_state[c])

    def exchange(i, src, dst, peer):
        return pltpu.make_async_remote_copy(
            src_ref=src, dst_ref=dst, send_sem=e_send.at[i], recv_sem=e_recv.at[i],
            device_id=(peer, M), device_id_type=MESH,
        )

    other = holder(span + 1 - 2 * half_row, char)
    swap = [exchange(0, s_own, s_pair, other), exchange(1, d_own, d_pair, other)]
    for one in swap:
        one.start()

    gates(3)
    gate_in[char] = gate_own[pl.ds(pl.multiple_of(place * FR, FR), FR)]
    inside(0, 6)

    for one in swap:
        one.wait_recv()
    upper = half_row == 1
    mine, theirs = s_last[...], s_pair[...].astype(F32)
    my_decay, their_decay = d_own[...], d_pair[...]
    late_decay = column(jnp.where(upper, my_decay, their_decay))
    s_row[...] = (late_decay * jnp.where(upper, theirs, mine) + jnp.where(upper, mine, theirs)).astype(BF)
    d_row[...] = my_decay * their_decay

    def to_row(k):
        if k == 2:
            peer = holder(lax.rem(span + 4, CH), char)
        else:
            peer = lax.rem(x + k, NX) * NZ + lax.rem(z + (2 if k == 1 else NZ - 2), NZ)
        return [
            pltpu.make_async_remote_copy(
                src_ref=src, dst_ref=dst.at[x], send_sem=sent.at[k], recv_sem=recv.at[x],
                device_id=(peer, M), device_id_type=MESH,
            )
            for src, dst, sent, recv in ((s_row, s_in, s_send, s_recv), (d_row, d_in, d_send, d_recv))
        ]

    for k in range(1, NX):
        @pl.when(x + k < NX)
        def _():
            for one in to_row(k):
                one.start()


    inside(6, CH)

    for k in range(NX - 1):
        @pl.when(k < x)
        def _():
            pltpu.make_async_copy(s_in.at[k], s_in.at[k], s_recv.at[k]).wait()
            pltpu.make_async_copy(d_in.at[k], d_in.at[k], d_recv.at[k]).wait()

    state = s_in[0].astype(F32)
    for k in range(1, NX - 1):
        state = state * column(d_in[k]) + s_in[k].astype(F32)
    state = jnp.where(upper, state * column(d_pair[...]) + s_pair[...].astype(F32), state)
    for h in range(2):
        rows = pl.ds(h * (ROWS // 2), ROWS // 2)
        full = attended[rows, :] + dot3(carried_q[rows, :], state)
        square = jnp.mean(full * full, axis=-1, keepdims=True)
        norm_own[rows, :] = (full * lax.rsqrt(square + 1e-06) * gain_row).astype(BF)

        @pl.loop(0, 4)
        def _(k):
            to = h * 4 + lax.rem(place + k, 4)

            @pl.when(to != place)
            def _():
                sent_rows = norm_own.at[pl.ds(pl.multiple_of(to * FR, FR), FR)]
                piece(sent_rows, norm_in.at[char], norm_sem, span * CH + to).start()

    norm_in[char] = norm_own[pl.ds(pl.multiple_of(place * FR, FR), FR)]
    wait_bytes(gate_in.at[pl.ds(0, CH - 1)], gate_sem.at[1])
    silu = gate_in[...].reshape(ROWS, 128).astype(F32)
    wait_bytes(norm_in.at[pl.ds(0, CH - 1)], norm_sem.at[1])
    normed = norm_in[...].reshape(ROWS, 128).astype(F32)
    mixed = dot(mix[...], norm_in[...].reshape(ROWS, 128))
    gat[M] = ((normed + mixed * inv_partners[...]) * silu).astype(BF)

    half = ROWS // 2

    def gated_part(slot, h, i, to):
        ref = gat.at[slot, pl.ds(h * half, half)]
        return pltpu.make_async_remote_copy(
            src_ref=ref, dst_ref=ref, send_sem=g_send.at[i], recv_sem=g_recv.at[i],
            device_id=(T, to), device_id_type=MESH,
        )

    def go(*args):
        send(gated_part(*args))

    def arrived(slot, h, i):
        gated_part(slot, h, i, sib).wait_recv()

    def along_x(m):
        to, j = m // 2, lax.rem(m, 2)
        return pltpu.make_async_remote_copy(
            src_ref=gbuf.at[m], dst_ref=xr.at[j, x], send_sem=x_send, recv_sem=x_recv.at[j],
            device_id=(to * NZ + z, M), device_id_type=MESH,
        )

    def produce(m, first=False):
        rows = gat[m]
        part = dot(rows, cot_v[...], ((0,), (0,))).reshape(8, 16, 256)
        gradf[m] = part
        gbuf[m] = part.astype(BF)

        @pl.when(m // 2 != x)
        def _():
            along_x(m).start()

        term = dot(rows, ow_v[m])
        oacc[...] = term if first else oacc[...] + term

    go(M, 0, 2, right)
    go(M, 1, 5, left)
    go(M, 0, 0, sib)
    go(M, 1, 1, sib)
    go(M, 1, 3, right)
    go(M, 0, 4, left)
    produce(M, True)
    arrived(left, 0, 2)
    go(left, 0, 6, right)
    go(left, 0, 8, sib)
    arrived(right, 1, 5)
    go(right, 1, 7, left)
    go(right, 1, 11, sib)
    arrived(sib, 0, 0)
    arrived(sib, 1, 1)
    arrived(left, 1, 3)
    go(left, 1, 9, sib)
    arrived(right, 0, 4)
    go(right, 0, 10, sib)
    produce(left)
    produce(right)
    arrived(opp, 0, 6)
    go(opp, 0, 12, sib)
    arrived(opp, 1, 7)
    go(opp, 1, 13, sib)
    produce(opp)
    produce(sib)
    for yy, i in ((left_y, 8), (right_y, 10), (opp_y, 12)):
        slot = 2 * yy + 1 - core
        arrived(slot, 0, i)
        arrived(slot, 1, i + 1)
        produce(slot)

    out_v[...] = oacc[...].astype(BF)
    store = pltpu.make_async_copy(out_v, out, out_sem.at[0])
    store.start()

    for j in (core, 1 - core):
        wait_bytes(xr.at[j, pl.ds(0, NX - 1)], x_recv.at[j])
        total = gradf[2 * x + j]
        for d in range(1, NX):
            total += xr[j, lax.rem(x + d, NX)].astype(F32)
        owners = pl.ds(j * 8, 8)
        zf[owners] = total
        zbuf[owners] = total.astype(BF)

        @pl.loop(0, 8)
        def _(k):
            to = j * 8 + lax.rem(z + k, 8)

            @pl.when(to != z)
            def _():
                piece(zbuf.at[to], zr.at[z], z_sem, x * NZ + to).start()

    wait_bytes(zr.at[pl.ds(0, NZ - 1)], z_sem.at[1])
    total = zf[z]
    for k in range(1, NZ):
        total += zr[lax.rem(z + k, NZ)].astype(F32)
    grad_v[...] = total
    last_store = pltpu.make_async_copy(grad_v, grad, out_sem.at[1])
    last_store.start()

    for d in range(NX):
        @pl.when(at_home)
        def _():
            wait_bytes(rx.at[d, pl.ds(0, CH - 1)], a_send)

        @pl.when(jnp.logical_not(at_home))
        def _():
            wait_bytes(rx.at[d], a_send)

    wait_bytes(res_in.at[pl.ds(0, CH - 1)], r_sem.at[0])
    for one in pending:
        one.wait_send()
    for one in swap:
        one.wait_send()
    for k in range(1, NX):
        @pl.when(x + k < NX)
        def _():
            for one in to_row(k):
                one.wait_send()

    wait_bytes(gate_in.at[pl.ds(0, CH - 1)], gate_sem.at[0])
    wait_bytes(norm_in.at[pl.ds(0, CH - 1)], norm_sem.at[0])
    for j in range(2):
        wait_bytes(xr.at[j, pl.ds(0, NX - 1)], x_send)
    wait_bytes(zbuf.at[pl.ds(0, NZ - 1)], z_sem.at[0])
    store.wait()
    last_store.wait()


def local(
    observations, contact, resets, q_weight, k_weight, v_weight, decay_weight, gate_weight,
    decay_bias, norm_gain, out_weight, out_cotangent,
):
    features = jnp.swapaxes(observations[0], 0, 1)
    weights = [
        w.reshape(8, MP, 32, 128) for w in (q_weight, k_weight, v_weight, decay_weight, gate_weight)
    ]
    vm = pltpu.VMEM
    dma = pltpu.SemaphoreType.DMA
    scratch = [
        vm((FR, CH), jnp.int32), vm((CH, FR), jnp.int32), vm((MP, 8, 32, 640), BF), vm((1, 128), F32),
        vm((1, 128), F32), vm((MP, 128, 256), BF), vm((ROWS, 256), BF),
        vm((NX, CH, 32, WAVE), BF), vm((MP, ROWS, 256), BF), vm((ROWS, 640), F32), vm((ROWS, 128), F32),
        vm((CH, 1, 128), F32), vm((CH, 1, 128), F32), vm((CH, FR, 128), F32), vm((CH, 1, FR), F32),
        vm((len(LEVELS) + 1, FR, FR), F32), vm((len(LEVELS) * FR, FR), BF),
        vm((ROWS, ROWS), BF), vm((ROWS, 128), F32),
        vm((CH, 128, 128), F32), vm((CH, 1, 128), F32), vm((128, 128), F32),
        vm((128, 128), BF), vm((1, 128), F32), vm((128, 128), BF), vm((1, 128), F32),
        vm((128, 128), BF), vm((1, 128), F32), vm((NX, 128, 128), BF), vm((NX, 1, 128), F32), vm((ROWS, 128), F32), vm((ROWS, 128), F32),
        vm((ROWS, 128), BF), vm((CH, FR, 128), BF), vm((ROWS, 128), BF), vm((CH, FR, 128), BF),
        vm((MP, ROWS, 128), BF), vm((ROWS, 256), F32), vm((MP, 8, 16, 256), F32),
        vm((MP, 8, 16, 256), BF), vm((2, NX, 8, 16, 256), BF), vm((NZ, 16, 256), F32),
        vm((NZ, 16, 256), BF), vm((NZ, 16, 256), BF), vm((ROWS, 256), BF), vm((16, 256), F32),
        dma((6,)), dma, dma((2,)), dma, dma((NX,)), dma((NX, 7)), dma((NX, 7)), dma((2,)),
        dma((2,)), dma((2,)), dma((NX,)), dma((NX,)), dma((NX,)), dma((NX,)), dma((2,)), dma((2,)), dma((14,)), dma((14,)), dma, dma((2,)), dma((2,)),
    ]
    following, weight_grad = pl.pallas_call(
        kernel,
        out_shape=(
            jax.ShapeDtypeStruct((ROWS, 256), BF),
            jax.ShapeDtypeStruct((16, 256), F32),
        ),
        in_specs=[pl.BlockSpec(memory_space=pltpu.HBM)] * 12,
        out_specs=(pl.BlockSpec(memory_space=pltpu.HBM),) * 2,
        scratch_shapes=scratch,
        compiler_params=pltpu.CompilerParams(
            collective_id=0, has_side_effects=True, vmem_limit_bytes=60 * 2**20
        ),
    )(
        features, contact.reshape(FR, CH), resets, *weights, decay_bias, norm_gain,
        out_weight.reshape(MP, 128, 256), out_cotangent.reshape(ROWS, 256),
    )
    return following.reshape(CH, FR, 256), weight_grad


def solution(mesh):
    placed = (
        P("tm", None, "mp"),
        P("tm", None, None),
        P(None, "tm"),
        P(None, "mp"),
        P(None, "mp"),
        P(None, "mp"),
        P(None, "mp"),
        P(None, "mp"),
        P("mp", None),
        P("mp", None),
        P(None, "mp"),
        P(None, "tm", "mp"),
    )
    return jax.shard_map(
        local,
        mesh=mesh,
        in_specs=placed,
        out_specs=(P(None, "tm", "mp"), P("tm", "mp")),
        check_vma=False,
    )
```
